32 devices in a mesh: row: 16 (over z, y, x), col: 2 (over core).
Axes of the slice: x: 2, y: 2, z: 4, core: 2. Of those that a mesh axis runs over, the one named last changes fastest.
Arguments:
- pair_trunk: bfloat16 [256, 256, 128], P('row', 'col'), may hold values from -6 to 6
- pair_gain: float32 [128], replicated, may hold values from 0.25 to 1.75
- pair_weight: bfloat16 [4, 128], replicated, may hold values from -0.5 to 0.5
- atom_features: bfloat16 [16, 2048, 128], P(None, ('row', 'col')), may hold values from -6 to 6
- atom_gain: float32 [128], replicated, may hold values from 0.25 to 1.75
- attn_weights: bfloat16 [4, 128, 128], replicated, may hold values from -0.5 to 0.5
- token_atoms: int32 [16, 16], replicated, may hold values from 1 to 24, 128 in all within a row
- window_starts: int32 [64], P(('row', 'col')), may hold values from 0 to 1920, as said below
- out_cotangent: bfloat16 [16, 2048, 128], P(None, ('row', 'col')), may hold values from -6 to 6
Outputs:
- updated: bfloat16 [16, 2048, 128], P(None, ('row', 'col'))
- grad_atoms: float32 [16, 2048, 128], P(None, ('row', 'col'))
- grad_pair: bfloat16 [256, 256, 128], P('row', 'col')
- grad_attn_weights: float32 [4, 128, 128], replicated
- grad_atom_gain: float32 [128], replicated
- grad_pair_weight: float32 [4, 128], replicated
- grad_pair_gain: float32 [128], replicated
The draws below stay inside these ranges and needn't reach their ends.
Inputs may be any that keep to these rules, and one draw needn't show every extreme that they name: `window_starts`: query block b's window starts within 16 atoms of 32 * b + 32/2 - 128/2, clipped to the atoms; the first block's window starts at 0 and the last block's at 1920.
All inputs are finite; a program needn't handle non-finite values.
Results may differ from the reference program's by a relative error of at most 0.012.
Values may be sent and summed in bfloat16 or wider, within the bound.
A program may use at most 128 MiB of HBM per device.

```python
import math
import jax
import jax.numpy as jnp
import numpy as np
from jax import lax

WIDTH = 128
HEADS = 4
PAIR_WIDTH = 128
QBLOCK = 32
WINDOW = 128
MOST = 24
SAMPLES = 16
TOKENS = 256
BAND = 16
ATOMS = 2048
ATOM_BAND = 128
NBLOCKS = 64
N_ROW = 16
N_COL = 2


def draw_window_starts(key, part):
    blocks = jnp.arange(NBLOCKS, dtype=jnp.int32)
    jitter = jax.random.randint(key, (NBLOCKS,), -(QBLOCK // 2), QBLOCK // 2 + 1, dtype=jnp.int32)
    raw = QBLOCK * blocks + QBLOCK // 2 - WINDOW // 2 + jitter
    return jnp.clip(raw, 0, ATOMS - WINDOW).astype(jnp.int32)


def levels(rng, dims, cuts, smallest, high):
    factor_of, own = 1.0, jax.random.fold_in(rng, 6)
    for axis_at, blocks in cuts:
        steps = jnp.exp(jax.random.uniform(jax.random.fold_in(own, axis_at), (blocks,), jnp.float32, smallest / len(cuts), high / len(cuts)))
        factor_of = factor_of * jnp.repeat(steps, dims[axis_at] // blocks).reshape([-1 if axis == axis_at else 1 for axis in range(len(dims))])
    return factor_of


def split_up(count, total, limit, skew):
    loads = [(1 << 20) // math.isqrt(standing ** skew) + 1 for standing in range(2, count + 1)]
    spare, holding = total - limit - (count - 1), [1] * (count - 1)
    while spare > 0:
        free = [i for i in range(count - 1) if holding[i] < limit]
        pool, remaining = sum([loads[i] for i in free]), spare
        for i in free:
            addition = min(limit - holding[i], max(1, remaining * loads[i] // pool), spare)
            holding[i] = holding[i] + addition
            spare = spare - addition
    return np.array([limit] + holding)


def uneven(own_key, number_of, total, bound, skew):
    if number_of == 2:
        one = jax.random.randint(own_key, (), max(1, total - bound), min(bound, total - 1) + 1)
        return jnp.stack([one, total - one])
    sizes = jnp.asarray(split_up(number_of, total, bound, skew), jnp.int32)
    couples = (number_of - 1) // 2
    donor, receiver = sizes[1:1 + 2 * couples:2], sizes[2:2 + 2 * couples:2]
    room = jnp.minimum(donor - 1, bound - receiver)
    passed = jax.random.randint(jax.random.fold_in(own_key, 1), (couples,), 0, 1 << 20) % (room + 1)
    sizes = sizes.at[1:1 + 2 * couples:2].set(donor - passed).at[2:2 + 2 * couples:2].set(receiver + passed)
    return sizes[jax.random.permutation(jax.random.fold_in(own_key, 2), number_of)]


def gaussian(key, shape, scale, limit, shards=(), kind=jnp.bfloat16):
    level = levels(key, shape, shards, -0.22, 0.18) if shards else 1.0
    drawn = jax.random.normal(key, shape, jnp.float32) * scale * level
    return jnp.minimum(jnp.maximum(drawn, -limit), limit).astype(kind)


def setup_inputs(seed: int = 0) -> dict:
    key_of = jax.random.split(jax.random.key(seed), 10)
    return {
        "pair_trunk": gaussian(key_of[0], (TOKENS, TOKENS, PAIR_WIDTH), 1.0, 6.0, ((0, 16), (1, 2))),
        "pair_gain": jnp.clip(1.0 + 0.15 * jax.random.normal(key_of[1], (PAIR_WIDTH,), jnp.float32), 0.25, 1.75),
        "pair_weight": gaussian(key_of[2], (HEADS, PAIR_WIDTH), PAIR_WIDTH ** -0.5, 0.5),
        "atom_features": gaussian(key_of[3], (SAMPLES, ATOMS, WIDTH), 1.0, 6.0, ((1, 32),)),
        "atom_gain": jnp.clip(1.0 + 0.15 * jax.random.normal(key_of[4], (WIDTH,), jnp.float32), 0.25, 1.75),
        "attn_weights": gaussian(key_of[5], (4, WIDTH, WIDTH), WIDTH ** -0.5, 0.5),
        "token_atoms": jax.vmap(lambda own: uneven(own, BAND, ATOM_BAND, MOST, 1))(jax.random.split(key_of[6], N_ROW)).reshape((N_ROW, BAND)).astype(jnp.int32),
        "window_starts": draw_window_starts(jax.random.fold_in(key_of[9], 71), 0),
        "out_cotangent": gaussian(key_of[8], (SAMPLES, ATOMS, WIDTH), 1.0, 6.0, ((1, 32),)),
    }


def layer_norm(values, gain):
    center = values - lax.optimization_barrier(jnp.mean(values, axis=-1, keepdims=True))
    spread = lax.optimization_barrier(jnp.mean(center * center, axis=-1, keepdims=True))
    return center * lax.rsqrt(spread + 1e-05) * gain

def pair_norm(block, gain):
    return layer_norm(block.astype(jnp.float32), gain)

def pair_forward(pair_block, pair_gain, pair_weight):
    normed, norm_back = jax.vjp(pair_norm, pair_block, pair_gain)
    normed_bf = normed.astype(jnp.bfloat16)
    bias = jnp.einsum('ijc,hc->hij', normed_bf, pair_weight, preferred_element_type=jnp.float32)
    return (bias.astype(jnp.bfloat16), normed_bf, norm_back)

def pair_backward(grad_bias, normed_bf, pair_weight, norm_back):
    grad_weight = jnp.einsum('hij,ijc->hc', grad_bias, normed_bf, preferred_element_type=jnp.float32)
    grad_normed = jnp.einsum('hij,hc->ijc', grad_bias, pair_weight, preferred_element_type=jnp.float32)
    grad_block, grad_gain = norm_back(grad_normed)
    return (grad_block, grad_gain, grad_weight)

def project_atoms(atoms_f, atom_gain, attn_weights):
    normed, norm_back = jax.vjp(layer_norm, atoms_f, atom_gain)
    normed_bf = normed.astype(jnp.bfloat16)
    projected = jnp.einsum('sac,pcd->psad', normed_bf, attn_weights[:3], preferred_element_type=jnp.float32).astype(jnp.bfloat16)
    return (projected[0], projected[1:], normed_bf, norm_back)

def project_back(grad_proj, normed_bf, attn_weights, norm_back):
    grad_weight = jnp.einsum('sac,psad->pcd', normed_bf, grad_proj, preferred_element_type=jnp.float32)
    grad_normed = jnp.einsum('psad,pcd->sac', grad_proj, attn_weights[:3], preferred_element_type=jnp.float32)
    grad_in, grad_gain = norm_back(grad_normed)
    return (grad_in, grad_gain, grad_weight)

def block_attention(query_blk, keys_ext, offset, tile):
    heads = tile.shape[0]
    samples, rows_q, width = query_blk.shape
    head_dim = width // heads
    window = tile.shape[2]
    kv_win = lax.dynamic_slice_in_dim(keys_ext, offset, window, 2).astype(jnp.bfloat16)
    q_heads = query_blk.reshape(samples, rows_q, heads, head_dim)
    k_heads = kv_win[0].reshape(samples, window, heads, head_dim)
    v_heads = kv_win[1].reshape(samples, window, heads, head_dim)
    scores = jnp.einsum('sqhd,skhd->shqk', q_heads, k_heads, preferred_element_type=jnp.float32) / math.sqrt(head_dim) + tile[None]
    scores = scores - lax.stop_gradient(lax.optimization_barrier(jnp.max(scores, axis=-1, keepdims=True)))
    weights = jnp.exp(scores)
    probs = (weights / lax.optimization_barrier(jnp.sum(weights, axis=-1, keepdims=True))).astype(jnp.bfloat16)
    mixed = jnp.einsum('shqk,skhd->sqhd', probs, v_heads, preferred_element_type=jnp.float32)
    return mixed.reshape(samples, rows_q, width).astype(jnp.bfloat16)

def device_attention(queries, keys_ext, offsets, tiles):
    samples, count, width = queries.shape
    nblk = offsets.shape[0]
    blocks = queries.reshape(samples, nblk, count // nblk, width)
    mixed = jax.vmap(block_attention, in_axes=(1, None, 0, 0), out_axes=1)(blocks, keys_ext, offsets, tiles)
    return mixed.reshape(samples, count, width)

def residual_out(mixed, atoms_f, attn_weights):
    moved = jnp.einsum('sac,cd->sad', mixed, attn_weights[3], preferred_element_type=jnp.float32)
    return (atoms_f + moved).astype(jnp.bfloat16)

def residual_back(cotangent, mixed, attn_weights):
    grad_weight = jnp.einsum('sac,sad->cd', mixed, cotangent, preferred_element_type=jnp.float32)
    grad_mixed = jnp.einsum('sad,cd->sac', cotangent, attn_weights[3], preferred_element_type=jnp.float32)
    return (grad_mixed.astype(jnp.bfloat16), grad_weight)

def token_index(atom_ids, token_atoms, band_atoms):
    band_id = atom_ids // band_atoms
    local_id = atom_ids - band_id * band_atoms
    totals = jnp.cumsum(token_atoms, axis=1)
    rows_sel = totals[band_id]
    found = lax.optimization_barrier(jnp.sum((rows_sel <= local_id[..., None]).astype(jnp.int32), axis=-1))
    return (band_id * token_atoms.shape[1] + found).astype(jnp.int32)

def reference(pair_trunk, pair_gain, pair_weight, atom_features, atom_gain, attn_weights, token_atoms, window_starts, out_cotangent):
    device_count = N_ROW * N_COL
    half = WINDOW // 2
    per_dev = ATOMS // device_count
    atoms_f = atom_features.astype(jnp.float32)
    pair_blocks = pair_trunk.reshape(N_ROW, BAND, TOKENS, PAIR_WIDTH)
    bias_rows = lax.map(lambda blk: pair_forward(blk, pair_gain, pair_weight)[0], pair_blocks)
    bias_full = bias_rows.transpose(1, 0, 2, 3).reshape(HEADS, TOKENS, TOKENS).astype(jnp.float32)
    query_tok = token_index(jnp.arange(ATOMS, dtype=jnp.int32), token_atoms, ATOM_BAND).reshape(NBLOCKS, QBLOCK)
    key_ids = window_starts[:, None] + jnp.arange(WINDOW, dtype=jnp.int32)[None, :]
    key_tok = token_index(key_ids, token_atoms, ATOM_BAND)
    dev_first = jnp.arange(device_count, dtype=jnp.int32) * per_dev - half
    offsets = (window_starts.reshape(device_count, per_dev // QBLOCK) - dev_first[:, None]).astype(jnp.int32)
    queries, keyvals, normed_bf, norm_back = project_atoms(atoms_f, atom_gain, attn_weights)
    parts = keyvals.astype(jnp.float32).reshape(2, SAMPLES, device_count, per_dev, WIDTH)
    zero_part = jnp.zeros((2, SAMPLES, 1, per_dev, WIDTH), jnp.float32)
    before = jnp.concatenate([zero_part, parts[:, :, :-1]], axis=2)[:, :, :, per_dev - half:, :]
    after = jnp.concatenate([parts[:, :, 1:], zero_part], axis=2)[:, :, :, :half, :]
    extended = jnp.concatenate([before, parts, after], axis=3).transpose(2, 0, 1, 3, 4)
    query_dev = queries.reshape(SAMPLES, device_count, per_dev, WIDTH).transpose(1, 0, 2, 3)

    def attend_all(query_in, ext_in, bias_in):
        tiles = bias_in[:, query_tok[:, :, None], key_tok[:, None, :]].transpose(1, 0, 2, 3)
        tiles = tiles.reshape(device_count, per_dev // QBLOCK, HEADS, QBLOCK, WINDOW)
        mixed_dev = lax.map(lambda items: device_attention(items[0], items[1], items[2], items[3]), (query_in, ext_in, offsets, tiles))
        return mixed_dev.transpose(1, 0, 2, 3).reshape(SAMPLES, ATOMS, WIDTH)
    mixed, attend_back = jax.vjp(attend_all, query_dev, extended, bias_full)
    updated = residual_out(mixed, atoms_f, attn_weights)
    grad_mixed, grad_w_out = residual_back(out_cotangent, mixed, attn_weights)
    grad_qdev, grad_ext, grad_bias = attend_back(grad_mixed)
    inner = grad_ext[:, :, :, half:half + per_dev]
    upper = grad_ext[:, :, :, half + per_dev:]
    lower = grad_ext[:, :, :, :half]
    zero_rim = jnp.zeros((1,) + upper.shape[1:], jnp.float32)
    from_below = jnp.concatenate([zero_rim, upper[:-1]], axis=0)
    from_above = jnp.concatenate([lower[1:], zero_rim], axis=0)
    inner = inner.at[:, :, :, :half].add(from_below)
    inner = inner.at[:, :, :, per_dev - half:].add(from_above)
    grad_kv = inner.transpose(1, 2, 0, 3, 4).reshape(2, SAMPLES, ATOMS, WIDTH).astype(jnp.bfloat16)
    grad_q = grad_qdev.transpose(1, 0, 2, 3).reshape(SAMPLES, ATOMS, WIDTH).astype(jnp.bfloat16)
    grad_proj = jnp.concatenate([grad_q[None], grad_kv], axis=0)
    grad_in, grad_atom_gain, grad_w_proj = project_back(grad_proj, normed_bf, attn_weights, norm_back)
    grad_atoms = out_cotangent.astype(jnp.float32) + grad_in
    grad_weights = jnp.concatenate([grad_w_proj, grad_w_out[None]], axis=0)
    grad_bias_rows = grad_bias.astype(jnp.bfloat16).reshape(HEADS, N_ROW, BAND, TOKENS).transpose(1, 0, 2, 3)

    def pair_back(items):
        blk, cot = items
        unused, normed_p, back_p = pair_forward(blk, pair_gain, pair_weight)
        return pair_backward(cot, normed_p, pair_weight, back_p)
    grad_pair_rows, gain_terms, weight_terms = lax.map(pair_back, (pair_blocks, grad_bias_rows))
    grad_pair = grad_pair_rows.reshape(TOKENS, TOKENS, PAIR_WIDTH)
    return (updated, grad_atoms, grad_pair, grad_weights, grad_atom_gain, lax.optimization_barrier(jnp.sum(weight_terms, axis=0)), lax.optimization_barrier(jnp.sum(gain_terms, axis=0)))
```

```python
import functools
import math

import jax
import jax.numpy as jnp
from jax import lax
from jax.experimental import pallas as pl
from jax.experimental.pallas import tpu as pltpu
from jax.sharding import PartitionSpec as P

WINDOW = 128
EPS = 1e-05
MESH = pl.DeviceIdType.MESH
F32 = jnp.float32
BF16 = jnp.bfloat16
NT = (((1,), (1,)), ((), ()))
NN = (((1,), (0,)), ((), ()))
TN = (((0,), (0,)), ((), ()))
MASKED = -1e30
GROUP = 4
PAIRED = 2


def dot(a, b, dims):
    return lax.dot_general(a, b, dims, preferred_element_type=F32)


def iota(shape, dim):
    return lax.broadcasted_iota(jnp.int32, shape, dim)


def normalised(x):
    x = x.astype(F32)
    center = x - jnp.mean(x, axis=-1, keepdims=True)
    rstd = lax.rsqrt(jnp.mean(center * center, axis=-1, keepdims=True) + EPS)
    return center * rstd, rstd


def norm_back(grad, gain, xhat, rstd):
    scaled = grad * gain
    first = jnp.mean(scaled, axis=-1, keepdims=True)
    second = jnp.mean(scaled * xhat, axis=-1, keepdims=True)
    return rstd * (scaled - first - xhat * second)


def fold8(x):
    return jnp.sum(x.reshape(x.shape[0] // 8, 8, x.shape[1]), axis=0)


def kernel(
    n_row, n_col,
    trunk, pair_gain, pair_weight, atoms, atom_gain, weights, token_atoms, starts, cot,
    updated, grad_atoms, grad_pair, grad_w, grad_again, grad_pweight, grad_pgain,
    halo, q_s, k_ext, v_ext, n_ext, xhat_s, rstd_s, gmix, mixed_s, dq_s, dkv_s,
    dn_own, dn_out, dn_in, tile, dt_acc, ok_s, oq_s, hmask_s, wrep_s, pxhat, prstd,
    bias_all, g_out, g_in, rs_out, rs_in, cb, ag, sm, sc,
    halo_ss, halo_rs, bias_ss, bias_rs, dn_ss, dn_rs, g_ss, g_rs,
    rs_ss, rs_rs, cb_ss, cb_rs, ag_ss, ag_rs, sm_ss, sm_rs, sc_ss, sc_rs,
):
    row = lax.axis_index("row")
    col = lax.axis_index("col")
    n_dev = n_row * n_col
    me = row * n_col + col
    up = lax.rem(me + 1, n_dev)
    down = lax.rem(me + n_dev - 1, n_dev)
    up_id = (up // n_col, lax.rem(up, n_col))
    down_id = (down // n_col, lax.rem(down, n_col))
    samples, count, width = atoms.shape
    band, cols, _ = trunk.shape
    heads = pair_weight.shape[0]
    head_dim = width // heads
    total = cols * n_col
    lanes = wrep_s.shape[0]
    ext = count + WINDOW
    half = WINDOW // 2
    hq = heads * count
    scale = 1.0 / math.sqrt(head_dim)
    band_atoms = count * n_col
    first = me * count

    def row_peer(d):
        return lax.rem(row + d, n_row)

    def col_peer(d):
        return lax.rem(col + d, n_col)

    barrier = pltpu.get_barrier_semaphore()
    pl.semaphore_signal(barrier, inc=1, device_id=up_id, device_id_type=MESH)
    pl.semaphore_signal(barrier, inc=1, device_id=down_id, device_id_type=MESH)

    @pl.loop(1, n_row)
    def _(d):
        pl.semaphore_signal(barrier, inc=1, device_id=(row_peer(d), col), device_id_type=MESH)

    @pl.loop(1, n_col)
    def _(d):
        pl.semaphore_signal(barrier, inc=1, device_id=(row, col_peer(d)), device_id_type=MESH)

    again = atom_gain[...]
    pgain = pair_gain[...]

    wqkv = jnp.concatenate([weights[0], weights[1], weights[2]], axis=1)
    wkv = jnp.concatenate([weights[1], weights[2]], axis=1)

    @pl.loop(0, samples // GROUP)
    def _(c):
        some = pl.ds(c * GROUP, GROUP)
        flat = (GROUP * count, width)
        cube = (GROUP, count, width)
        xhat, rstd = normalised(atoms[some].reshape(flat))
        normed = (xhat * again).astype(BF16)
        proj = dot(normed, wqkv, NN).astype(BF16)
        xhat_s[some] = xhat.reshape(cube)
        rstd_s[some] = rstd.reshape(GROUP, count, 1)
        n_ext[some, half : half + count] = normed.reshape(cube)
        q_s[some] = proj[:, :width].reshape(cube)
        k_ext[some, half : half + count] = proj[:, width : 2 * width].reshape(cube)
        v_ext[some, half : half + count] = proj[:, 2 * width :].reshape(cube)
        gmix[some] = dot(cot[some].reshape(flat), weights[3], NT).astype(BF16).reshape(cube)

    pl.semaphore_wait(barrier, n_row + n_col)

    def halo_copy(d, where):
        return pltpu.make_async_remote_copy(
            src_ref=atoms, dst_ref=halo.at[d], send_sem=halo_ss.at[d], recv_sem=halo_rs.at[d],
            device_id=where, device_id_type=MESH)

    halos = [halo_copy(0, up_id), halo_copy(1, down_id)]
    for copy in halos:
        copy.start()

    lane_row = iota((lanes, width), 0)
    wrep = jnp.zeros((lanes, width), F32)
    for h in range(heads):
        wrep = jnp.where(lane_row // band == h, pair_weight[h : h + 1, :].astype(F32), wrep)
    wrep_s[...] = wrep.astype(BF16)

    def pair_rows(i):
        return jnp.where(lane_row % band == i, wrep_s[...].astype(F32), 0.0).astype(BF16)

    def forward_step(i, acc):
        xhat, rstd = normalised(trunk[i])
        pxhat[i] = xhat
        prstd[i] = rstd
        return acc + dot((xhat * pgain).astype(BF16), pair_rows(i), NT)

    bias = lax.fori_loop(0, band, forward_step, jnp.zeros((cols, lanes), F32), unroll=2)
    bias_all[col] = bias.astype(BF16)

    def bias_copy(peer, slot):
        return pltpu.make_async_remote_copy(
            src_ref=bias_all.at[col], dst_ref=bias_all.at[slot], send_sem=bias_ss.at[peer],
            recv_sem=bias_rs.at[slot], device_id=(row, peer), device_id_type=MESH)

    @pl.loop(1, n_col)
    def _(d):
        bias_copy(col_peer(d), col).start()

    table = token_atoms[...].astype(F32).astype(BF16)

    def bounds(size, token_of, band_of, band_row):
        token = token_of(iota((band, size), 1))
        at = iota((band, size), 0)
        own = iota((n_row, size), 0) == band_of(iota((n_row, size), 1))
        out = []
        for strict in (True, False):
            below = (at < token) if strict else (at <= token)
            sums = dot(table, jnp.where(below, 1.0, 0.0).astype(BF16), NN)
            inner = jnp.sum(jnp.where(own, sums, 0.0), axis=0, keepdims=True)
            out.append(inner.astype(jnp.int32) + band_row(iota((1, size), 1)) * band_atoms)
        return out

    low, high = bounds(total, lambda j: j % band, lambda j: j // band, lambda j: j // band)
    key_atom = first - half + iota((ext, total), 0)
    ok_s[...] = jnp.where((key_atom >= low) & (key_atom < high), 1.0, 0.0).astype(BF16)
    low, high = bounds(lanes, lambda l: l % band, lambda l: l * 0 + row, lambda l: l * 0 + row)
    sub = iota((hq, lanes), 0)
    query_atom = first + sub % count
    same_head = (sub // count) == (iota((hq, lanes), 1) // band)
    oq_s[...] = jnp.where(
        same_head & (query_atom >= low) & (query_atom < high), 1.0, 0.0).astype(BF16)
    hmask_s[...] = jnp.where(
        iota((hq, width), 0) // count == iota((hq, width), 1) // head_dim, 1.0, 0.0).astype(BF16)

    for d, copy in enumerate(halos):
        copy.wait()
        base = d * (half + count)

        @pl.loop(0, samples // GROUP)
        def _(c, d=d, base=base):
            some = pl.ds(c * GROUP, GROUP)
            cube = (GROUP, half, width)
            side = halo[d, some]
            xhat, _r = normalised(side.reshape(GROUP * half, width))
            normed = (xhat * again).astype(BF16)
            proj = dot(normed, wkv, NN).astype(BF16)
            n_ext[some, base : base + half] = normed.reshape(cube)
            k_ext[some, base : base + half] = proj[:, :width].reshape(cube)
            v_ext[some, base : base + half] = proj[:, width:].reshape(cube)

    @pl.loop(1, n_col)
    def _(d):
        peer = col_peer(d)
        bias_copy(peer, peer).wait()

    spread = dot(ok_s[...], bias_all[...].reshape(total, lanes), NN).astype(BF16)
    block = (iota((ext, hq), 1) % count) // (count // starts.shape[0])
    offset = jnp.zeros((ext, hq), jnp.int32)
    for b in range(starts.shape[0]):
        offset = jnp.where(block == b, starts[b] - (first - half), offset)
    place = iota((ext, hq), 0) - offset
    tile[...] = jnp.where(
        (place >= 0) & (place < WINDOW), dot(spread, oq_s[...], NT), MASKED)
    dt_acc[...] = jnp.zeros_like(dt_acc)

    def dn_copy(d, it, where):
        some = pl.ds(it * PAIRED, PAIRED)
        return pltpu.make_async_remote_copy(
            src_ref=dn_out.at[d, some], dst_ref=dn_in.at[d, some], send_sem=dn_ss.at[d, it],
            recv_sem=dn_rs.at[d, it], device_id=where, device_id_type=MESH)

    def by_head(full):
        masked = full * hmask_s[...].astype(F32)
        out = masked[:count]
        for h in range(1, heads):
            out = out + masked[h * count : (h + 1) * count]
        return out

    def spread_heads(x):
        return jnp.concatenate([x] * heads, axis=0) * hmask_s[...]

    @pl.loop(0, samples // PAIRED)
    def _(it):
        added = None
        for u in range(PAIRED):
            s = it * PAIRED + u
            k, v = k_ext[s], v_ext[s]
            qbd = spread_heads(q_s[s])
            gbd = spread_heads(gmix[s])
            scores = dot(k, qbd, NT) * scale + tile[...]
            grown = jnp.exp(scores - jnp.max(scores, axis=0, keepdims=True))
            probs = grown * (1.0 / jnp.sum(grown, axis=0, keepdims=True))
            probs_bf = probs.astype(BF16)
            mixed_s[s] = by_head(dot(probs_bf, v, TN)).astype(BF16)
            gprobs = dot(v, gbd, NT).astype(BF16).astype(F32)
            weighed = probs * gprobs
            gscores = weighed - probs * jnp.sum(weighed, axis=0, keepdims=True)
            added = gscores if added is None else added + gscores
            gs_bf = (gscores * scale).astype(BF16)
            gq = by_head(dot(gs_bf, k, TN)).astype(BF16)
            gk = dot(gs_bf, qbd, NN).astype(BF16)
            gv = dot(probs_bf, gbd, NN).astype(BF16)
            dq_s[s] = gq
            dkv_s[s, :, :width] = gk
            dkv_s[s, :, width:] = gv
            gn = dot(gk, weights[1], NT) + dot(gv, weights[2], NT)
            dn_out[0, s] = gn[:half].astype(BF16)
            dn_out[1, s] = gn[half + count :].astype(BF16)
            dn_own[s] = gn[half : half + count] + dot(gq, weights[0], NT)
        dt_acc[...] += added
        dn_copy(0, it, down_id).start()
        dn_copy(1, it, up_id).start()

    by_query = dot(dt_acc[...].astype(BF16), oq_s[...], NN).astype(BF16)
    g_out[...] = dot(ok_s[...], by_query, TN).astype(BF16).reshape(n_col, cols, lanes)

    def g_copy(peer, slot):
        return pltpu.make_async_remote_copy(
            src_ref=g_out.at[peer], dst_ref=g_in.at[slot], send_sem=g_ss.at[peer],
            recv_sem=g_rs.at[slot], device_id=(row, peer), device_id_type=MESH)

    @pl.loop(1, n_col)
    def _(d):
        g_copy(col_peer(d), col).start()

    g_in[col] = g_out[col]

    rows_all = samples * count
    share = rs_out.shape[1]
    own_n = n_ext[:, half : half + count].reshape(rows_all, width)
    per = width // share
    gwq = dot(own_n, dq_s[...].reshape(rows_all, width), TN)
    gwkv = dot(n_ext[...].reshape(samples * ext, width),
               dkv_s[...].reshape(samples * ext, 2 * width), TN)
    mixed_all = mixed_s[...].reshape(rows_all, width)
    gwo = dot(mixed_all, cot[...].reshape(rows_all, width), TN)
    for p, value in enumerate((gwq, gwkv[:, :width], gwkv[:, width:], gwo)):
        rs_out[p * per : (p + 1) * per] = value.astype(BF16).reshape(per, share, width)

    def rs_copy(peer, slot):
        return pltpu.make_async_remote_copy(
            src_ref=rs_out.at[peer], dst_ref=rs_in.at[slot], send_sem=rs_ss.at[peer],
            recv_sem=rs_rs.at[slot], device_id=(peer, col), device_id_type=MESH)

    @pl.loop(1, n_row)
    def _(d):
        rs_copy(row_peer(d), row).start()

    rs_in[row] = rs_out[row]

    @pl.loop(0, samples // GROUP)
    def _(c):
        some = pl.ds(c * GROUP, GROUP)
        moved = dot(mixed_s[some].reshape(GROUP * count, width), weights[3], NN)
        updated[some] = (atoms[some].astype(F32) + moved.reshape(GROUP, count, width)).astype(BF16)

    @pl.loop(1, n_col)
    def _(d):
        peer = col_peer(d)
        g_copy(peer, peer).wait()

    grad_bias = g_in[0].astype(F32)
    for c in range(1, n_col):
        grad_bias = grad_bias + g_in[c].astype(F32)
    grad_bias_t = grad_bias.T.astype(BF16)
    grad_bias = grad_bias.astype(BF16)

    def backward_step(i, carry):
        gain_acc, w_acc = carry
        xhat = pxhat[i]
        grad = dot(grad_bias, pair_rows(i), NN)
        normed = (xhat * pgain).astype(BF16)
        gain_acc = gain_acc + fold8(grad * xhat)
        w_acc = w_acc + jnp.where(lane_row % band == i, dot(grad_bias_t, normed, NN), 0.0)
        grad_pair[i] = norm_back(grad, pgain, xhat, prstd[i]).astype(BF16)
        return gain_acc, w_acc

    pgain_acc, w_acc = lax.fori_loop(
        0, band, backward_step,
        (jnp.zeros((8, width), F32), jnp.zeros((lanes, width), F32)), unroll=2)

    @pl.loop(1, n_row)
    def _(d):
        peer = row_peer(d)
        rs_copy(peer, peer).wait()

    part = rs_in[0].astype(F32)
    for r in range(1, n_row):
        part = part + rs_in[r].astype(F32)
    cb[col] = part

    def cb_copy(peer, slot):
        return pltpu.make_async_remote_copy(
            src_ref=cb.at[col], dst_ref=cb.at[slot], send_sem=cb_ss.at[peer],
            recv_sem=cb_rs.at[slot], device_id=(row, peer), device_id_type=MESH)

    @pl.loop(1, n_col)
    def _(d):
        cb_copy(col_peer(d), col).start()

    @pl.loop(0, samples // PAIRED)
    def _(it):
        dn_copy(0, it, down_id).wait()
        dn_copy(1, it, up_id).wait()

    def atom_step(c, gain_acc):
        some = pl.ds(c * GROUP, GROUP)
        flat = (GROUP * count, width)
        cube = (GROUP, count, width)
        grad = (dn_own[some] + dn_in[0, some].astype(F32) + dn_in[1, some].astype(F32)).reshape(flat)
        xhat = xhat_s[some].reshape(flat)
        back = norm_back(grad, again, xhat, rstd_s[some].reshape(GROUP * count, 1))
        grad_atoms[some] = cot[some].astype(F32) + back.reshape(cube)
        return gain_acc + fold8(grad * xhat)

    again_acc = lax.fori_loop(0, samples // GROUP, atom_step, jnp.zeros((8, width), F32))

    @pl.loop(1, n_col)
    def _(d):
        peer = col_peer(d)
        cb_copy(peer, peer).wait()

    whole = cb[0]
    for c in range(1, n_col):
        whole = whole + cb[c]
    ag[row] = whole.astype(BF16)

    def ag_copy(peer, slot):
        return pltpu.make_async_remote_copy(
            src_ref=ag.at[row], dst_ref=ag.at[slot], send_sem=ag_ss.at[peer],
            recv_sem=ag_rs.at[slot], device_id=(peer, col), device_id_type=MESH)

    small = [jnp.sum(again_acc, axis=0, keepdims=True), jnp.sum(pgain_acc, axis=0, keepdims=True)]
    for h in range(heads):
        small.append(jnp.sum(w_acc[h * band : (h + 1) * band], axis=0, keepdims=True))
    small.append(jnp.zeros((8 - len(small), width), F32))
    sm[row] = jnp.concatenate(small, axis=0)

    def sm_copy(peer, slot):
        return pltpu.make_async_remote_copy(
            src_ref=sm.at[row], dst_ref=sm.at[slot], send_sem=sm_ss.at[peer],
            recv_sem=sm_rs.at[slot], device_id=(peer, col), device_id_type=MESH)

    @pl.loop(1, n_row)
    def _(d):
        sm_copy(row_peer(d), row).start()
        ag_copy(row_peer(d), row).start()

    @pl.loop(1, n_row)
    def _(d):
        peer = row_peer(d)
        sm_copy(peer, peer).wait()

    small_part = sm[0]
    for r in range(1, n_row):
        small_part = small_part + sm[r]
    sc[col] = small_part

    def sc_copy(peer, slot):
        return pltpu.make_async_remote_copy(
            src_ref=sc.at[col], dst_ref=sc.at[slot], send_sem=sc_ss.at[peer],
            recv_sem=sc_rs.at[slot], device_id=(row, peer), device_id_type=MESH)

    @pl.loop(1, n_col)
    def _(d):
        sc_copy(col_peer(d), col).start()

    @pl.loop(1, n_row)
    def _(d):
        peer = row_peer(d)
        ag_copy(peer, peer).wait()

    for p in range(4):
        grad_w[p] = ag[p * per : (p + 1) * per].reshape(width, width).astype(F32)

    @pl.loop(1, n_col)
    def _(d):
        peer = col_peer(d)
        sc_copy(peer, peer).wait()

    sums = sc[0]
    for c in range(1, n_col):
        sums = sums + sc[c]
    grad_again[...] = sums[0:1]
    grad_pgain[...] = sums[1:2]
    grad_pweight[...] = sums[2 : 2 + heads]


def per_device(
    n_row, n_col,
    pair_trunk, pair_gain, pair_weight, atom_features, atom_gain, attn_weights, token_atoms,
    window_starts, out_cotangent,
):
    band, cols, width = pair_trunk.shape
    samples, count, _ = atom_features.shape
    heads = pair_weight.shape[0]
    total = cols * n_col
    lanes = max(128, heads * band)
    ext = count + WINDOW
    half = WINDOW // 2
    hq = heads * count
    share = 4 * width // n_row
    vmem = pl.BlockSpec(memory_space=pltpu.VMEM)
    smem = pl.BlockSpec(memory_space=pltpu.SMEM)
    dma = pltpu.SemaphoreType.DMA
    steps = samples // PAIRED
    scratch = [
        ((2, samples, count, width), BF16),
        ((samples, count, width), BF16),
        ((samples, ext, width), BF16),
        ((samples, ext, width), BF16),
        ((samples, ext, width), BF16),
        ((samples, count, width), F32),
        ((samples, count, 1), F32),
        ((samples, count, width), BF16),
        ((samples, count, width), BF16),
        ((samples, count, width), BF16),
        ((samples, ext, 2 * width), BF16),
        ((samples, count, width), F32),
        ((2, samples, half, width), BF16),
        ((2, samples, half, width), BF16),
        ((ext, hq), F32),
        ((ext, hq), F32),
        ((ext, total), BF16),
        ((hq, lanes), BF16),
        ((hq, width), BF16),
        ((lanes, width), BF16),
        ((band, cols, width), F32),
        ((band, cols, 1), F32),
        ((n_col, cols, lanes), BF16),
        ((n_col, cols, lanes), BF16),
        ((n_col, cols, lanes), BF16),
        ((n_row, share, width), BF16),
        ((n_row, share, width), BF16),
        ((n_col, share, width), F32),
        ((n_row, share, width), BF16),
        ((n_row, 8, width), F32),
        ((n_col, 8, width), F32),
    ]
    sems = [(2,), (2,), (n_col,), (n_col,), (2, steps), (2, steps), (n_col,), (n_col,),
            (n_row,), (n_row,), (n_col,), (n_col,), (n_row,), (n_row,), (n_row,), (n_row,),
            (n_col,), (n_col,)]
    outs = pl.pallas_call(
        functools.partial(kernel, n_row, n_col),
        out_shape=[
            jax.ShapeDtypeStruct((samples, count, width), BF16),
            jax.ShapeDtypeStruct((samples, count, width), F32),
            jax.ShapeDtypeStruct((band, cols, width), BF16),
            jax.ShapeDtypeStruct((4, width, width), F32),
            jax.ShapeDtypeStruct((1, width), F32),
            jax.ShapeDtypeStruct((heads, width), F32),
            jax.ShapeDtypeStruct((1, width), F32),
        ],
        in_specs=[vmem] * 7 + [smem, vmem],
        out_specs=[vmem] * 7,
        scratch_shapes=[pltpu.VMEM(shape, kind) for shape, kind in scratch]
        + [dma(shape) for shape in sems],
        compiler_params=pltpu.CompilerParams(
            collective_id=0, has_side_effects=True, vmem_limit_bytes=48 << 20),
    )(
        pair_trunk, pair_gain.reshape(1, width), pair_weight, atom_features,
        atom_gain.reshape(1, width), attn_weights, token_atoms, window_starts, out_cotangent,
    )
    return (outs[0], outs[1], outs[2], outs[3], outs[4].reshape(width), outs[5],
            outs[6].reshape(width))


def solution(mesh):
    atoms_at = P(None, ("row", "col"), None)
    pairs_at = P("row", "col", None)
    return jax.shard_map(
        functools.partial(per_device, mesh.shape["row"], mesh.shape["col"]),
        mesh=mesh,
        in_specs=(pairs_at, P(), P(), atoms_at, P(), P(), P(), P(("row", "col")), atoms_at),
        out_specs=(atoms_at, atoms_at, pairs_at, P(), P(), P(), P()),
        check_vma=False,
    )
```

```python
import functools
import math

import jax
import jax.numpy as jnp
from jax import lax
from jax.experimental import pallas as pl
from jax.experimental.pallas import tpu as pltpu
from jax.sharding import PartitionSpec as P

WINDOW = 128
EPS = 1e-05
MESH = pl.DeviceIdType.MESH
F32 = jnp.float32
BF16 = jnp.bfloat16
NT = (((1,), (1,)), ((), ()))
NN = (((1,), (0,)), ((), ()))
TN = (((0,), (0,)), ((), ()))
MASKED = -1e30
GROUP = 4
PAIRED = 2


def dot(a, b, dims):
    return lax.dot_general(a, b, dims, preferred_element_type=F32)


def iota(shape, dim):
    return lax.broadcasted_iota(jnp.int32, shape, dim)


def normalised(x):
    x = x.astype(F32)
    center = x - jnp.mean(x, axis=-1, keepdims=True)
    rstd = lax.rsqrt(jnp.mean(center * center, axis=-1, keepdims=True) + EPS)
    return center * rstd, rstd


def norm_back(grad, gain, xhat, rstd):
    scaled = grad * gain
    first = jnp.mean(scaled, axis=-1, keepdims=True)
    second = jnp.mean(scaled * xhat, axis=-1, keepdims=True)
    return rstd * (scaled - first - xhat * second)


def fold8(x):
    return jnp.sum(x.reshape(x.shape[0] // 8, 8, x.shape[1]), axis=0)


def kernel(
    n_row, n_col,
    trunk_h, pgain_h, pweight_h, atoms_h, again_h, weights_h, tokens_h, starts_h, cot_h,
    updated, grad_atoms, grad_pair, grad_w, grad_again, grad_pweight, grad_pgain,
    trunk, pair_gain, pair_weight, atoms, atom_gain, weights, token_atoms, cot, starts,
    halo, q_s, k_ext, v_ext, n_ext, xhat_s, rstd_s, gmix, mixed_s, dq_s, dkv_s,
    dn_own, dn_out, dn_in, tile, dt_acc, ok_s, oq_s, hmask_s, wrep_s, pxhat, prstd,
    bias_all, g_out, g_in, rs_out, rs_in, cb, ag, sm, sc,
    in_s, halo_ss, halo_rs, bias_ss, bias_rs, dn_ss, dn_rs, g_ss, g_rs,
    rs_ss, rs_rs, cb_ss, cb_rs, ag_ss, ag_rs, sm_ss, sm_rs, sc_ss, sc_rs,
):
    row = lax.axis_index("row")
    col = lax.axis_index("col")
    n_dev = n_row * n_col
    me = row * n_col + col
    up = lax.rem(me + 1, n_dev)
    down = lax.rem(me + n_dev - 1, n_dev)
    up_id = (up // n_col, lax.rem(up, n_col))
    down_id = (down // n_col, lax.rem(down, n_col))
    samples, count, width = atoms.shape
    band, cols, _ = trunk.shape
    heads = pair_weight.shape[0]
    head_dim = width // heads
    total = cols * n_col
    lanes = wrep_s.shape[0]
    ext = count + WINDOW
    half = WINDOW // 2
    hq = heads * count
    scale = 1.0 / math.sqrt(head_dim)
    band_atoms = count * n_col
    first = me * count

    def row_peer(d):
        return lax.rem(row + d, n_row)

    def col_peer(d):
        return lax.rem(col + d, n_col)

    loads = [
        pltpu.make_async_copy(source, target, in_s.at[n])
        for n, (source, target) in enumerate((
            (trunk_h, trunk), (pgain_h, pair_gain), (pweight_h, pair_weight),
            (again_h, atom_gain), (atoms_h, atoms), (weights_h, weights), (cot_h, cot),
            (tokens_h, token_atoms), (starts_h, starts)))
    ]
    barrier = pltpu.get_barrier_semaphore()
    pl.semaphore_signal(barrier, inc=1, device_id=up_id, device_id_type=MESH)
    pl.semaphore_signal(barrier, inc=1, device_id=down_id, device_id_type=MESH)

    @pl.loop(1, n_row)
    def _(d):
        pl.semaphore_signal(barrier, inc=1, device_id=(row_peer(d), col), device_id_type=MESH)

    @pl.loop(1, n_col)
    def _(d):
        pl.semaphore_signal(barrier, inc=1, device_id=(row, col_peer(d)), device_id_type=MESH)

    for copy in loads:
        copy.start()
    pl.semaphore_wait(barrier, n_row + n_col)

    def halo_copy(d, it, where):
        some = pl.ds(it * PAIRED, PAIRED)
        return pltpu.make_async_remote_copy(
            src_ref=atoms_h.at[some], dst_ref=halo.at[d, some], send_sem=halo_ss.at[d, it],
            recv_sem=halo_rs.at[d, it], device_id=where, device_id_type=MESH)

    @pl.loop(0, samples // PAIRED)
    def _(it):
        halo_copy(0, it, up_id).start()
        halo_copy(1, it, down_id).start()

    for copy in loads[:4]:
        copy.wait()
    again = atom_gain[...]
    pgain = pair_gain[...]

    lane_row = iota((lanes, width), 0)
    wrep = jnp.zeros((lanes, width), F32)
    for h in range(heads):
        wrep = jnp.where(lane_row // band == h, pair_weight[h : h + 1, :].astype(F32), wrep)
    wrep_s[...] = wrep.astype(BF16)

    def pair_rows(i):
        return jnp.where(lane_row % band == i, wrep_s[...].astype(F32), 0.0).astype(BF16)

    def forward_step(i, acc):
        xhat, rstd = normalised(trunk[i])
        pxhat[i] = xhat
        prstd[i] = rstd
        return acc + dot((xhat * pgain).astype(BF16), pair_rows(i), NT)

    bias = lax.fori_loop(0, band, forward_step, jnp.zeros((cols, lanes), F32), unroll=2)
    bias_all[col] = bias.astype(BF16)

    def bias_copy(peer, slot):
        return pltpu.make_async_remote_copy(
            src_ref=bias_all.at[col], dst_ref=bias_all.at[slot], send_sem=bias_ss.at[peer],
            recv_sem=bias_rs.at[slot], device_id=(row, peer), device_id_type=MESH)

    @pl.loop(1, n_col)
    def _(d):
        bias_copy(col_peer(d), col).start()

    for copy in loads[4:]:
        copy.wait()

    wqkv = jnp.concatenate([weights[0], weights[1], weights[2]], axis=1)
    wkv = jnp.concatenate([weights[1], weights[2]], axis=1)

    @pl.loop(0, samples // GROUP)
    def _(c):
        some = pl.ds(c * GROUP, GROUP)
        flat = (GROUP * count, width)
        cube = (GROUP, count, width)
        xhat, rstd = normalised(atoms[some].reshape(flat))
        normed = (xhat * again).astype(BF16)
        proj = dot(normed, wqkv, NN).astype(BF16)
        xhat_s[some] = xhat.reshape(cube)
        rstd_s[some] = rstd.reshape(GROUP, count, 1)
        n_ext[some, half : half + count] = normed.reshape(cube)
        q_s[some] = proj[:, :width].reshape(cube)
        k_ext[some, half : half + count] = proj[:, width : 2 * width].reshape(cube)
        v_ext[some, half : half + count] = proj[:, 2 * width :].reshape(cube)
        gmix[some] = dot(cot[some].reshape(flat), weights[3], NT).astype(BF16).reshape(cube)

    table = token_atoms[...].astype(F32).astype(BF16)

    def bounds(size, token_of, band_of, band_row):
        token = token_of(iota((band, size), 1))
        at = iota((band, size), 0)
        own = iota((n_row, size), 0) == band_of(iota((n_row, size), 1))
        out = []
        for strict in (True, False):
            below = (at < token) if strict else (at <= token)
            sums = dot(table, jnp.where(below, 1.0, 0.0).astype(BF16), NN)
            inner = jnp.sum(jnp.where(own, sums, 0.0), axis=0, keepdims=True)
            out.append(inner.astype(jnp.int32) + band_row(iota((1, size), 1)) * band_atoms)
        return out

    low, high = bounds(total, lambda j: j % band, lambda j: j // band, lambda j: j // band)
    key_atom = first - half + iota((ext, total), 0)
    ok_s[...] = jnp.where((key_atom >= low) & (key_atom < high), 1.0, 0.0).astype(BF16)
    low, high = bounds(lanes, lambda l: l % band, lambda l: l * 0 + row, lambda l: l * 0 + row)
    sub = iota((hq, lanes), 0)
    query_atom = first + sub % count
    same_head = (sub // count) == (iota((hq, lanes), 1) // band)
    oq_s[...] = jnp.where(
        same_head & (query_atom >= low) & (query_atom < high), 1.0, 0.0).astype(BF16)
    hmask_s[...] = jnp.where(
        iota((hq, width), 0) // count == iota((hq, width), 1) // head_dim, 1.0, 0.0).astype(BF16)

    @pl.loop(1, n_col)
    def _(d):
        peer = col_peer(d)
        bias_copy(peer, peer).wait()

    spread = dot(ok_s[...], bias_all[...].reshape(total, lanes), NN).astype(BF16)
    block = (iota((ext, hq), 1) % count) // (count // starts.shape[0])
    offset = jnp.zeros((ext, hq), jnp.int32)
    for b in range(starts.shape[0]):
        offset = jnp.where(block == b, starts[b] - (first - half), offset)
    place = iota((ext, hq), 0) - offset
    tile[...] = jnp.where(
        (place >= 0) & (place < WINDOW), dot(spread, oq_s[...], NT), MASKED)
    dt_acc[...] = jnp.zeros_like(dt_acc)

    def dn_copy(d, it, where):
        some = pl.ds(it * PAIRED, PAIRED)
        return pltpu.make_async_remote_copy(
            src_ref=dn_out.at[d, some], dst_ref=dn_in.at[d, some], send_sem=dn_ss.at[d, it],
            recv_sem=dn_rs.at[d, it], device_id=where, device_id_type=MESH)

    def by_head(full):
        masked = full * hmask_s[...].astype(F32)
        out = masked[:count]
        for h in range(1, heads):
            out = out + masked[h * count : (h + 1) * count]
        return out

    def spread_heads(x):
        return jnp.concatenate([x] * heads, axis=0) * hmask_s[...]

    @pl.loop(0, samples // PAIRED)
    def _(it):
        halo_copy(0, it, up_id).wait()
        halo_copy(1, it, down_id).wait()
        some = pl.ds(it * PAIRED, PAIRED)
        cube = (PAIRED, half, width)
        for d in range(2):
            base = d * (half + count)
            xhat, _r = normalised(halo[d, some].reshape(PAIRED * half, width))
            normed = (xhat * again).astype(BF16)
            proj = dot(normed, wkv, NN).astype(BF16)
            n_ext[some, base : base + half] = normed.reshape(cube)
            k_ext[some, base : base + half] = proj[:, :width].reshape(cube)
            v_ext[some, base : base + half] = proj[:, width:].reshape(cube)
        added = None
        for u in range(PAIRED):
            s = it * PAIRED + u
            k, v = k_ext[s], v_ext[s]
            qbd = spread_heads(q_s[s])
            gbd = spread_heads(gmix[s])
            scores = dot(k, qbd, NT) * scale + tile[...]
            grown = jnp.exp(scores - jnp.max(scores, axis=0, keepdims=True))
            probs = grown * (1.0 / jnp.sum(grown, axis=0, keepdims=True))
            probs_bf = probs.astype(BF16)
            mixed_s[s] = by_head(dot(probs_bf, v, TN)).astype(BF16)
            gprobs = dot(v, gbd, NT).astype(BF16).astype(F32)
            weighed = probs * gprobs
            gscores = weighed - probs * jnp.sum(weighed, axis=0, keepdims=True)
            added = gscores if added is None else added + gscores
            gs_bf = (gscores * scale).astype(BF16)
            gq = by_head(dot(gs_bf, k, TN)).astype(BF16)
            gk = dot(gs_bf, qbd, NN).astype(BF16)
            gv = dot(probs_bf, gbd, NN).astype(BF16)
            dq_s[s] = gq
            dkv_s[s, :, :width] = gk
            dkv_s[s, :, width:] = gv
            gn = dot(gk, weights[1], NT) + dot(gv, weights[2], NT)
            dn_out[0, s] = gn[:half].astype(BF16)
            dn_out[1, s] = gn[half + count :].astype(BF16)
            dn_own[s] = gn[half : half + count] + dot(gq, weights[0], NT)
        dt_acc[...] += added
        dn_copy(0, it, down_id).start()
        dn_copy(1, it, up_id).start()

    by_query = dot(dt_acc[...].astype(BF16), oq_s[...], NN).astype(BF16)
    g_out[...] = dot(ok_s[...], by_query, TN).astype(BF16).reshape(n_col, cols, lanes)

    def g_copy(peer, slot):
        return pltpu.make_async_remote_copy(
            src_ref=g_out.at[peer], dst_ref=g_in.at[slot], send_sem=g_ss.at[peer],
            recv_sem=g_rs.at[slot], device_id=(row, peer), device_id_type=MESH)

    @pl.loop(1, n_col)
    def _(d):
        g_copy(col_peer(d), col).start()

    g_in[col] = g_out[col]

    rows_all = samples * count
    share = rs_out.shape[1]
    own_n = n_ext[:, half : half + count].reshape(rows_all, width)
    per = width // share
    gwq = dot(own_n, dq_s[...].reshape(rows_all, width), TN)
    gwkv = dot(n_ext[...].reshape(samples * ext, width),
               dkv_s[...].reshape(samples * ext, 2 * width), TN)
    mixed_all = mixed_s[...].reshape(rows_all, width)
    gwo = dot(mixed_all, cot[...].reshape(rows_all, width), TN)
    for p, value in enumerate((gwq, gwkv[:, :width], gwkv[:, width:], gwo)):
        rs_out[p * per : (p + 1) * per] = value.astype(BF16).reshape(per, share, width)

    def rs_copy(peer, slot):
        return pltpu.make_async_remote_copy(
            src_ref=rs_out.at[peer], dst_ref=rs_in.at[slot], send_sem=rs_ss.at[peer],
            recv_sem=rs_rs.at[slot], device_id=(peer, col), device_id_type=MESH)

    @pl.loop(1, n_row)
    def _(d):
        rs_copy(row_peer(d), row).start()

    rs_in[row] = rs_out[row]

    @pl.loop(0, samples // GROUP)
    def _(c):
        some = pl.ds(c * GROUP, GROUP)
        moved = dot(mixed_s[some].reshape(GROUP * count, width), weights[3], NN)
        updated[some] = (atoms[some].astype(F32) + moved.reshape(GROUP, count, width)).astype(BF16)

    @pl.loop(1, n_col)
    def _(d):
        peer = col_peer(d)
        g_copy(peer, peer).wait()

    grad_bias = g_in[0].astype(F32)
    for c in range(1, n_col):
        grad_bias = grad_bias + g_in[c].astype(F32)
    grad_bias_t = grad_bias.T.astype(BF16)
    grad_bias = grad_bias.astype(BF16)

    def backward_step(i, carry):
        gain_acc, w_acc = carry
        xhat = pxhat[i]
        grad = dot(grad_bias, pair_rows(i), NN)
        normed = (xhat * pgain).astype(BF16)
        gain_acc = gain_acc + fold8(grad * xhat)
        w_acc = w_acc + jnp.where(lane_row % band == i, dot(grad_bias_t, normed, NN), 0.0)
        grad_pair[i] = norm_back(grad, pgain, xhat, prstd[i]).astype(BF16)
        return gain_acc, w_acc

    pgain_acc, w_acc = lax.fori_loop(
        0, band, backward_step,
        (jnp.zeros((8, width), F32), jnp.zeros((lanes, width), F32)), unroll=2)

    @pl.loop(1, n_row)
    def _(d):
        peer = row_peer(d)
        rs_copy(peer, peer).wait()

    part = rs_in[0].astype(F32)
    for r in range(1, n_row):
        part = part + rs_in[r].astype(F32)
    cb[col] = part

    def cb_copy(peer, slot):
        return pltpu.make_async_remote_copy(
            src_ref=cb.at[col], dst_ref=cb.at[slot], send_sem=cb_ss.at[peer],
            recv_sem=cb_rs.at[slot], device_id=(row, peer), device_id_type=MESH)

    @pl.loop(1, n_col)
    def _(d):
        cb_copy(col_peer(d), col).start()

    @pl.loop(0, samples // PAIRED)
    def _(it):
        dn_copy(0, it, down_id).wait()
        dn_copy(1, it, up_id).wait()

    def atom_step(c, gain_acc):
        some = pl.ds(c * GROUP, GROUP)
        flat = (GROUP * count, width)
        cube = (GROUP, count, width)
        grad = (dn_own[some] + dn_in[0, some].astype(F32) + dn_in[1, some].astype(F32)).reshape(flat)
        xhat = xhat_s[some].reshape(flat)
        back = norm_back(grad, again, xhat, rstd_s[some].reshape(GROUP * count, 1))
        grad_atoms[some] = cot[some].astype(F32) + back.reshape(cube)
        return gain_acc + fold8(grad * xhat)

    again_acc = lax.fori_loop(0, samples // GROUP, atom_step, jnp.zeros((8, width), F32))

    @pl.loop(1, n_col)
    def _(d):
        peer = col_peer(d)
        cb_copy(peer, peer).wait()

    whole = cb[0]
    for c in range(1, n_col):
        whole = whole + cb[c]
    ag[row] = whole.astype(BF16)

    def ag_copy(peer, slot):
        return pltpu.make_async_remote_copy(
            src_ref=ag.at[row], dst_ref=ag.at[slot], send_sem=ag_ss.at[peer],
            recv_sem=ag_rs.at[slot], device_id=(peer, col), device_id_type=MESH)

    small = [jnp.sum(again_acc, axis=0, keepdims=True), jnp.sum(pgain_acc, axis=0, keepdims=True)]
    for h in range(heads):
        small.append(jnp.sum(w_acc[h * band : (h + 1) * band], axis=0, keepdims=True))
    small.append(jnp.zeros((8 - len(small), width), F32))
    sm[row] = jnp.concatenate(small, axis=0)

    def sm_copy(peer, slot):
        return pltpu.make_async_remote_copy(
            src_ref=sm.at[row], dst_ref=sm.at[slot], send_sem=sm_ss.at[peer],
            recv_sem=sm_rs.at[slot], device_id=(peer, col), device_id_type=MESH)

    @pl.loop(1, n_row)
    def _(d):
        sm_copy(row_peer(d), row).start()
        ag_copy(row_peer(d), row).start()

    @pl.loop(1, n_row)
    def _(d):
        peer = row_peer(d)
        sm_copy(peer, peer).wait()

    small_part = sm[0]
    for r in range(1, n_row):
        small_part = small_part + sm[r]
    sc[col] = small_part

    def sc_copy(peer, slot):
        return pltpu.make_async_remote_copy(
            src_ref=sc.at[col], dst_ref=sc.at[slot], send_sem=sc_ss.at[peer],
            recv_sem=sc_rs.at[slot], device_id=(row, peer), device_id_type=MESH)

    @pl.loop(1, n_col)
    def _(d):
        sc_copy(col_peer(d), col).start()

    @pl.loop(1, n_row)
    def _(d):
        peer = row_peer(d)
        ag_copy(peer, peer).wait()

    for p in range(4):
        grad_w[p] = ag[p * per : (p + 1) * per].reshape(width, width).astype(F32)

    @pl.loop(1, n_col)
    def _(d):
        peer = col_peer(d)
        sc_copy(peer, peer).wait()

    sums = sc[0]
    for c in range(1, n_col):
        sums = sums + sc[c]
    grad_again[...] = sums[0:1]
    grad_pgain[...] = sums[1:2]
    grad_pweight[...] = sums[2 : 2 + heads]


def handover(*refs):
    count = (len(refs) - 1) // 2
    sems = refs[-1]
    copies = [
        pltpu.make_async_copy(refs[n], refs[count + n], sems.at[n]) for n in range(count)
    ]
    for copy in copies:
        copy.start()
    for copy in copies:
        copy.wait()


def per_device(
    n_row, n_col,
    pair_trunk, pair_gain, pair_weight, atom_features, atom_gain, attn_weights, token_atoms,
    window_starts, out_cotangent,
):
    band, cols, width = pair_trunk.shape
    samples, count, _ = atom_features.shape
    heads = pair_weight.shape[0]
    total = cols * n_col
    lanes = max(128, heads * band)
    ext = count + WINDOW
    half = WINDOW // 2
    hq = heads * count
    share = 4 * width // n_row
    vmem = pl.BlockSpec(memory_space=pltpu.VMEM)
    anywhere = pl.BlockSpec(memory_space=pl.ANY)
    dma = pltpu.SemaphoreType.DMA
    steps = samples // PAIRED
    hbm = pl.BlockSpec(memory_space=pltpu.HBM)
    args = [
        pair_trunk, pair_gain.reshape(1, width), pair_weight, atom_features,
        atom_gain.reshape(1, width), attn_weights, token_atoms, window_starts, out_cotangent,
    ]
    scratch = [(args[n].shape, args[n].dtype) for n in (0, 1, 2, 3, 4, 5, 6, 8)]
    later = [
        ((2, samples, count, width), BF16),
        ((samples, count, width), BF16),
        ((samples, ext, width), BF16),
        ((samples, ext, width), BF16),
        ((samples, ext, width), BF16),
        ((samples, count, width), F32),
        ((samples, count, 1), F32),
        ((samples, count, width), BF16),
        ((samples, count, width), BF16),
        ((samples, count, width), BF16),
        ((samples, ext, 2 * width), BF16),
        ((samples, count, width), F32),
        ((2, samples, half, width), BF16),
        ((2, samples, half, width), BF16),
        ((ext, hq), F32),
        ((ext, hq), F32),
        ((ext, total), BF16),
        ((hq, lanes), BF16),
        ((hq, width), BF16),
        ((lanes, width), BF16),
        ((band, cols, width), F32),
        ((band, cols, 1), F32),
        ((n_col, cols, lanes), BF16),
        ((n_col, cols, lanes), BF16),
        ((n_col, cols, lanes), BF16),
        ((n_row, share, width), BF16),
        ((n_row, share, width), BF16),
        ((n_col, share, width), F32),
        ((n_row, share, width), BF16),
        ((n_row, 8, width), F32),
        ((n_col, 8, width), F32),
    ]
    sems = [(9,), (2, steps), (2, steps), (n_col,), (n_col,), (2, steps), (2, steps), (n_col,), (n_col,),
            (n_row,), (n_row,), (n_col,), (n_col,), (n_row,), (n_row,), (n_row,), (n_row,),
            (n_col,), (n_col,)]
    outs = pl.pallas_call(
        functools.partial(kernel, n_row, n_col),
        out_shape=[
            jax.ShapeDtypeStruct((samples, count, width), BF16),
            jax.ShapeDtypeStruct((samples, count, width), F32),
            jax.ShapeDtypeStruct((band, cols, width), BF16),
            jax.ShapeDtypeStruct((4, width, width), F32),
            jax.ShapeDtypeStruct((1, width), F32),
            jax.ShapeDtypeStruct((heads, width), F32),
            jax.ShapeDtypeStruct((1, width), F32),
        ],
        in_specs=[hbm] * 9,
        out_specs=[vmem] * 7,
        scratch_shapes=[pltpu.VMEM(shape, kind) for shape, kind in scratch]
        + [pltpu.SMEM(window_starts.shape, jnp.int32)]
        + [pltpu.VMEM(shape, kind) for shape, kind in later]
        + [dma(shape) for shape in sems],
        compiler_params=pltpu.CompilerParams(
            collective_id=0, has_side_effects=True, vmem_limit_bytes=60 << 20),
    )(*args)
    outs = pl.pallas_call(
        handover,
        out_shape=[pltpu.HBM(out.shape, out.dtype) for out in outs],
        in_specs=[anywhere] * 7,
        out_specs=[anywhere] * 7,
        scratch_shapes=[dma((7,))],
    )(*outs)
    return (outs[0], outs[1], outs[2], outs[3], outs[4].reshape(width), outs[5],
            outs[6].reshape(width))


def solution(mesh):
    atoms_at = P(None, ("row", "col"), None)
    pairs_at = P("row", "col", None)
    return jax.shard_map(
        functools.partial(per_device, mesh.shape["row"], mesh.shape["col"]),
        mesh=mesh,
        in_specs=(pairs_at, P(), P(), atoms_at, P(), P(), P(), P(("row", "col")), atoms_at),
        out_specs=(atoms_at, atoms_at, pairs_at, P(), P(), P(), P()),
        check_vma=False,
    )
```

```python
import functools
import math

import jax
import jax.numpy as jnp
from jax import lax
from jax.experimental import pallas as pl
from jax.experimental.pallas import tpu as pltpu
from jax.sharding import PartitionSpec as P

WINDOW = 128
EPS = 1e-05
MESH = pl.DeviceIdType.MESH
F32 = jnp.float32
BF16 = jnp.bfloat16
NT = (((1,), (1,)), ((), ()))
NN = (((1,), (0,)), ((), ()))
TN = (((0,), (0,)), ((), ()))
MASKED = -1e30
GROUP = 4
PAIRED = 4


def dot(a, b, dims):
    return lax.dot_general(a, b, dims, preferred_element_type=F32)


def iota(shape, dim):
    return lax.broadcasted_iota(jnp.int32, shape, dim)


def normalised(x):
    x = x.astype(F32)
    center = x - jnp.mean(x, axis=-1, keepdims=True)
    rstd = lax.rsqrt(jnp.mean(center * center, axis=-1, keepdims=True) + EPS)
    return center * rstd, rstd


def norm_back(grad, gain, xhat, rstd):
    scaled = grad * gain
    first = jnp.mean(scaled, axis=-1, keepdims=True)
    second = jnp.mean(scaled * xhat, axis=-1, keepdims=True)
    return rstd * (scaled - first - xhat * second)


def fold8(x):
    return jnp.sum(x.reshape(x.shape[0] // 8, 8, x.shape[1]), axis=0)


def kernel(
    n_row, n_col,
    trunk_h, pgain_h, pweight_h, atoms_h, again_h, weights_h, tokens_h, starts_h, cot_h,
    updated, grad_atoms, grad_pair, grad_w, grad_again, grad_pweight, grad_pgain,
    trunk, pair_gain, pair_weight, atoms, atom_gain, weights, token_atoms, cot, starts,
    halo, q_s, k_ext, v_ext, n_ext, xhat_s, rstd_s, gmix, mixed_s, dq_s, dkv_s,
    dn_own, dn_out, dn_in, tile, dt_acc, ok_s, oq_s, hmask_s, wrep_s, pxhat, prstd,
    bias_all, g_out, g_in, rs_out, rs_in, cb, ag, sm, sc,
    in_s, halo_ss, halo_rs, bias_ss, bias_rs, dn_ss, dn_rs, g_ss, g_rs,
    rs_ss, rs_rs, cb_ss, cb_rs, ag_ss, ag_rs, sm_ss, sm_rs, sc_ss, sc_rs,
):
    row = lax.axis_index("row")
    col = lax.axis_index("col")
    n_dev = n_row * n_col
    me = row * n_col + col
    up = lax.rem(me + 1, n_dev)
    down = lax.rem(me + n_dev - 1, n_dev)
    up_id = (up // n_col, lax.rem(up, n_col))
    down_id = (down // n_col, lax.rem(down, n_col))
    samples, count, width = atoms.shape
    band, cols, _ = trunk.shape
    heads = pair_weight.shape[0]
    head_dim = width // heads
    total = cols * n_col
    lanes = wrep_s.shape[0]
    ext = count + WINDOW
    half = WINDOW // 2
    hq = heads * count
    scale = 1.0 / math.sqrt(head_dim)
    band_atoms = count * n_col
    first = me * count

    def row_peer(d):
        return lax.rem(row + d, n_row)

    def col_peer(d):
        return lax.rem(col + d, n_col)

    loads = [
        pltpu.make_async_copy(source, target, in_s.at[n])
        for n, (source, target) in enumerate((
            (trunk_h, trunk), (pgain_h, pair_gain), (pweight_h, pair_weight),
            (again_h, atom_gain), (atoms_h, atoms), (weights_h, weights), (cot_h, cot),
            (tokens_h, token_atoms), (starts_h, starts)))
    ]
    barrier = pltpu.get_barrier_semaphore()
    pl.semaphore_signal(barrier, inc=1, device_id=up_id, device_id_type=MESH)
    pl.semaphore_signal(barrier, inc=1, device_id=down_id, device_id_type=MESH)

    @pl.loop(1, n_row)
    def _(d):
        pl.semaphore_signal(barrier, inc=1, device_id=(row_peer(d), col), device_id_type=MESH)

    @pl.loop(1, n_col)
    def _(d):
        pl.semaphore_signal(barrier, inc=1, device_id=(row, col_peer(d)), device_id_type=MESH)

    for copy in loads:
        copy.start()
    pl.semaphore_wait(barrier, n_row + n_col)

    def halo_copy(d, it, where):
        some = pl.ds(it * PAIRED, PAIRED)
        return pltpu.make_async_remote_copy(
            src_ref=atoms_h.at[some], dst_ref=halo.at[d, some], send_sem=halo_ss.at[d, it],
            recv_sem=halo_rs.at[d, it], device_id=where, device_id_type=MESH)

    @pl.loop(0, samples // PAIRED)
    def _(it):
        halo_copy(0, it, up_id).start()
        halo_copy(1, it, down_id).start()

    for copy in loads[:4]:
        copy.wait()
    again = atom_gain[...]
    pgain = pair_gain[...]

    lane_row = iota((lanes, width), 0)
    wrep = jnp.zeros((lanes, width), F32)
    for h in range(heads):
        wrep = jnp.where(lane_row // band == h, pair_weight[h : h + 1, :].astype(F32), wrep)
    wrep_s[...] = wrep.astype(BF16)

    def pair_rows(i):
        return jnp.where(lane_row % band == i, wrep_s[...].astype(F32), 0.0).astype(BF16)

    def forward_step(i, acc):
        xhat, rstd = normalised(trunk[i])
        pxhat[i] = xhat
        prstd[i] = rstd
        return acc + dot((xhat * pgain).astype(BF16), pair_rows(i), NT)

    bias = lax.fori_loop(0, band, forward_step, jnp.zeros((cols, lanes), F32), unroll=2)
    bias_all[col] = bias.astype(BF16)

    def bias_copy(peer, slot):
        return pltpu.make_async_remote_copy(
            src_ref=bias_all.at[col], dst_ref=bias_all.at[slot], send_sem=bias_ss.at[peer],
            recv_sem=bias_rs.at[slot], device_id=(row, peer), device_id_type=MESH)

    @pl.loop(1, n_col)
    def _(d):
        bias_copy(col_peer(d), col).start()

    for copy in loads[4:]:
        copy.wait()

    wqkv = jnp.concatenate([weights[0], weights[1], weights[2]], axis=1)
    wkv = jnp.concatenate([weights[1], weights[2]], axis=1)

    @pl.loop(0, samples // GROUP)
    def _(c):
        some = pl.ds(c * GROUP, GROUP)
        flat = (GROUP * count, width)
        cube = (GROUP, count, width)
        xhat, rstd = normalised(atoms[some].reshape(flat))
        normed = (xhat * again).astype(BF16)
        proj = dot(normed, wqkv, NN).astype(BF16)
        xhat_s[some] = xhat.reshape(cube)
        rstd_s[some] = rstd.reshape(GROUP, count, 1)
        n_ext[some, half : half + count] = normed.reshape(cube)
        q_s[some] = proj[:, :width].reshape(cube)
        k_ext[some, half : half + count] = proj[:, width : 2 * width].reshape(cube)
        v_ext[some, half : half + count] = proj[:, 2 * width :].reshape(cube)
        gmix[some] = dot(cot[some].reshape(flat), weights[3], NT).astype(BF16).reshape(cube)

    table = token_atoms[...].astype(F32).astype(BF16)

    def bounds(size, token_of, band_of, band_row):
        token = token_of(iota((band, size), 1))
        at = iota((band, size), 0)
        own = iota((n_row, size), 0) == band_of(iota((n_row, size), 1))
        out = []
        for strict in (True, False):
            below = (at < token) if strict else (at <= token)
            sums = dot(table, jnp.where(below, 1.0, 0.0).astype(BF16), NN)
            inner = jnp.sum(jnp.where(own, sums, 0.0), axis=0, keepdims=True)
            out.append(inner.astype(jnp.int32) + band_row(iota((1, size), 1)) * band_atoms)
        return out

    low, high = bounds(total, lambda j: j % band, lambda j: j // band, lambda j: j // band)
    key_atom = first - half + iota((ext, total), 0)
    ok_s[...] = jnp.where((key_atom >= low) & (key_atom < high), 1.0, 0.0).astype(BF16)
    low, high = bounds(lanes, lambda l: l % band, lambda l: l * 0 + row, lambda l: l * 0 + row)
    sub = iota((hq, lanes), 0)
    query_atom = first + sub % count
    same_head = (sub // count) == (iota((hq, lanes), 1) // band)
    oq_s[...] = jnp.where(
        same_head & (query_atom >= low) & (query_atom < high), 1.0, 0.0).astype(BF16)
    hmask_s[...] = jnp.where(
        iota((hq, width), 0) // count == iota((hq, width), 1) // head_dim, 1.0, 0.0).astype(BF16)

    @pl.loop(1, n_col)
    def _(d):
        peer = col_peer(d)
        bias_copy(peer, peer).wait()

    spread = dot(ok_s[...], bias_all[...].reshape(total, lanes), NN).astype(BF16)
    block = (iota((ext, hq), 1) % count) // (count // starts.shape[0])
    offset = jnp.zeros((ext, hq), jnp.int32)
    for b in range(starts.shape[0]):
        offset = jnp.where(block == b, starts[b] - (first - half), offset)
    place = iota((ext, hq), 0) - offset
    tile[...] = jnp.where(
        (place >= 0) & (place < WINDOW), dot(spread, oq_s[...], NT), MASKED)
    dt_acc[...] = jnp.zeros_like(dt_acc)

    def dn_copy(d, it, where):
        some = pl.ds(it * PAIRED, PAIRED)
        return pltpu.make_async_remote_copy(
            src_ref=dn_out.at[d, some], dst_ref=dn_in.at[d, some], send_sem=dn_ss.at[d, it],
            recv_sem=dn_rs.at[d, it], device_id=where, device_id_type=MESH)

    def by_head(full):
        masked = full * hmask_s[...].astype(F32)
        out = masked[:count]
        for h in range(1, heads):
            out = out + masked[h * count : (h + 1) * count]
        return out

    def spread_heads(x):
        return jnp.concatenate([x] * heads, axis=0) * hmask_s[...]

    @pl.loop(0, samples // PAIRED)
    def _(it):
        halo_copy(0, it, up_id).wait()
        halo_copy(1, it, down_id).wait()
        some = pl.ds(it * PAIRED, PAIRED)
        cube = (PAIRED, half, width)
        for d in range(2):
            base = d * (half + count)
            xhat, _r = normalised(halo[d, some].reshape(PAIRED * half, width))
            normed = (xhat * again).astype(BF16)
            proj = dot(normed, wkv, NN).astype(BF16)
            n_ext[some, base : base + half] = normed.reshape(cube)
            k_ext[some, base : base + half] = proj[:, :width].reshape(cube)
            v_ext[some, base : base + half] = proj[:, width:].reshape(cube)
        added = None
        for u in range(PAIRED):
            s = it * PAIRED + u
            k, v = k_ext[s], v_ext[s]
            qbd = spread_heads(q_s[s])
            gbd = spread_heads(gmix[s])
            scores = dot(k, qbd, NT) * scale + tile[...]
            grown = jnp.exp(scores - jnp.max(scores, axis=0, keepdims=True))
            probs = grown * (1.0 / jnp.sum(grown, axis=0, keepdims=True))
            probs_bf = probs.astype(BF16)
            mixed_s[s] = by_head(dot(probs_bf, v, TN)).astype(BF16)
            gprobs = dot(v, gbd, NT).astype(BF16).astype(F32)
            weighed = probs * gprobs
            gscores = weighed - probs * jnp.sum(weighed, axis=0, keepdims=True)
            added = gscores if added is None else added + gscores
            gs_bf = (gscores * scale).astype(BF16)
            gq = by_head(dot(gs_bf, k, TN)).astype(BF16)
            gk = dot(gs_bf, qbd, NN).astype(BF16)
            gv = dot(probs_bf, gbd, NN).astype(BF16)
            dq_s[s] = gq
            dkv_s[s, :, :width] = gk
            dkv_s[s, :, width:] = gv
            gn = dot(gk, weights[1], NT) + dot(gv, weights[2], NT)
            dn_out[0, s] = gn[:half].astype(BF16)
            dn_out[1, s] = gn[half + count :].astype(BF16)
            dn_own[s] = gn[half : half + count] + dot(gq, weights[0], NT)
        dt_acc[...] += added
        dn_copy(0, it, down_id).start()
        dn_copy(1, it, up_id).start()

    by_query = dot(dt_acc[...].astype(BF16), oq_s[...], NN).astype(BF16)
    g_out[...] = dot(ok_s[...], by_query, TN).astype(BF16).reshape(n_col, cols, lanes)

    def g_copy(peer, slot):
        return pltpu.make_async_remote_copy(
            src_ref=g_out.at[peer], dst_ref=g_in.at[slot], send_sem=g_ss.at[peer],
            recv_sem=g_rs.at[slot], device_id=(row, peer), device_id_type=MESH)

    @pl.loop(1, n_col)
    def _(d):
        g_copy(col_peer(d), col).start()

    g_in[col] = g_out[col]

    rows_all = samples * count
    share = rs_out.shape[1]
    own_n = n_ext[:, half : half + count].reshape(rows_all, width)
    per = width // share
    gwq = dot(own_n, dq_s[...].reshape(rows_all, width), TN)
    gwkv = dot(n_ext[...].reshape(samples * ext, width),
               dkv_s[...].reshape(samples * ext, 2 * width), TN)
    mixed_all = mixed_s[...].reshape(rows_all, width)
    gwo = dot(mixed_all, cot[...].reshape(rows_all, width), TN)
    for p, value in enumerate((gwq, gwkv[:, :width], gwkv[:, width:], gwo)):
        rs_out[p * per : (p + 1) * per] = value.astype(BF16).reshape(per, share, width)

    def rs_copy(peer, slot):
        return pltpu.make_async_remote_copy(
            src_ref=rs_out.at[peer], dst_ref=rs_in.at[slot], send_sem=rs_ss.at[peer],
            recv_sem=rs_rs.at[slot], device_id=(peer, col), device_id_type=MESH)

    @pl.loop(1, n_row)
    def _(d):
        rs_copy(row_peer(d), row).start()

    rs_in[row] = rs_out[row]

    @pl.loop(0, samples // GROUP)
    def _(c):
        some = pl.ds(c * GROUP, GROUP)
        moved = dot(mixed_s[some].reshape(GROUP * count, width), weights[3], NN)
        updated[some] = (atoms[some].astype(F32) + moved.reshape(GROUP, count, width)).astype(BF16)

    @pl.loop(1, n_col)
    def _(d):
        peer = col_peer(d)
        g_copy(peer, peer).wait()

    grad_bias = g_in[0].astype(F32)
    for c in range(1, n_col):
        grad_bias = grad_bias + g_in[c].astype(F32)
    grad_bias_t = grad_bias.T.astype(BF16)
    grad_bias = grad_bias.astype(BF16)

    def backward_step(i, carry):
        gain_acc, w_acc = carry
        xhat = pxhat[i]
        grad = dot(grad_bias, pair_rows(i), NN)
        normed = (xhat * pgain).astype(BF16)
        gain_acc = gain_acc + fold8(grad * xhat)
        w_acc = w_acc + jnp.where(lane_row % band == i, dot(grad_bias_t, normed, NN), 0.0)
        grad_pair[i] = norm_back(grad, pgain, xhat, prstd[i]).astype(BF16)
        return gain_acc, w_acc

    pgain_acc, w_acc = lax.fori_loop(
        0, band, backward_step,
        (jnp.zeros((8, width), F32), jnp.zeros((lanes, width), F32)), unroll=2)

    @pl.loop(1, n_row)
    def _(d):
        peer = row_peer(d)
        rs_copy(peer, peer).wait()

    part = rs_in[0].astype(F32)
    for r in range(1, n_row):
        part = part + rs_in[r].astype(F32)
    cb[col] = part

    def cb_copy(peer, slot):
        return pltpu.make_async_remote_copy(
            src_ref=cb.at[col], dst_ref=cb.at[slot], send_sem=cb_ss.at[peer],
            recv_sem=cb_rs.at[slot], device_id=(row, peer), device_id_type=MESH)

    @pl.loop(1, n_col)
    def _(d):
        cb_copy(col_peer(d), col).start()

    @pl.loop(0, samples // PAIRED)
    def _(it):
        dn_copy(0, it, down_id).wait()
        dn_copy(1, it, up_id).wait()

    def atom_step(c, gain_acc):
        some = pl.ds(c * GROUP, GROUP)
        flat = (GROUP * count, width)
        cube = (GROUP, count, width)
        grad = (dn_own[some] + dn_in[0, some].astype(F32) + dn_in[1, some].astype(F32)).reshape(flat)
        xhat = xhat_s[some].reshape(flat)
        back = norm_back(grad, again, xhat, rstd_s[some].reshape(GROUP * count, 1))
        grad_atoms[some] = cot[some].astype(F32) + back.reshape(cube)
        return gain_acc + fold8(grad * xhat)

    again_acc = lax.fori_loop(0, samples // GROUP, atom_step, jnp.zeros((8, width), F32))

    @pl.loop(1, n_col)
    def _(d):
        peer = col_peer(d)
        cb_copy(peer, peer).wait()

    whole = cb[0]
    for c in range(1, n_col):
        whole = whole + cb[c]
    ag[row] = whole.astype(BF16)

    def ag_copy(peer, slot):
        return pltpu.make_async_remote_copy(
            src_ref=ag.at[row], dst_ref=ag.at[slot], send_sem=ag_ss.at[peer],
            recv_sem=ag_rs.at[slot], device_id=(peer, col), device_id_type=MESH)

    small = [jnp.sum(again_acc, axis=0, keepdims=True), jnp.sum(pgain_acc, axis=0, keepdims=True)]
    for h in range(heads):
        small.append(jnp.sum(w_acc[h * band : (h + 1) * band], axis=0, keepdims=True))
    small.append(jnp.zeros((8 - len(small), width), F32))
    sm[row] = jnp.concatenate(small, axis=0)

    def sm_copy(peer, slot):
        return pltpu.make_async_remote_copy(
            src_ref=sm.at[row], dst_ref=sm.at[slot], send_sem=sm_ss.at[peer],
            recv_sem=sm_rs.at[slot], device_id=(peer, col), device_id_type=MESH)

    @pl.loop(1, n_row)
    def _(d):
        sm_copy(row_peer(d), row).start()
        ag_copy(row_peer(d), row).start()

    @pl.loop(1, n_row)
    def _(d):
        peer = row_peer(d)
        sm_copy(peer, peer).wait()

    small_part = sm[0]
    for r in range(1, n_row):
        small_part = small_part + sm[r]
    sc[col] = small_part

    def sc_copy(peer, slot):
        return pltpu.make_async_remote_copy(
            src_ref=sc.at[col], dst_ref=sc.at[slot], send_sem=sc_ss.at[peer],
            recv_sem=sc_rs.at[slot], device_id=(row, peer), device_id_type=MESH)

    @pl.loop(1, n_col)
    def _(d):
        sc_copy(col_peer(d), col).start()

    @pl.loop(1, n_row)
    def _(d):
        peer = row_peer(d)
        ag_copy(peer, peer).wait()

    for p in range(4):
        grad_w[p] = ag[p * per : (p + 1) * per].reshape(width, width).astype(F32)

    @pl.loop(1, n_col)
    def _(d):
        peer = col_peer(d)
        sc_copy(peer, peer).wait()

    sums = sc[0]
    for c in range(1, n_col):
        sums = sums + sc[c]
    grad_again[...] = sums[0:1]
    grad_pgain[...] = sums[1:2]
    grad_pweight[...] = sums[2 : 2 + heads]


def handover(*refs):
    count = (len(refs) - 2) // 3
    in_s, out_s = refs[-2:]
    arriving = [
        pltpu.make_async_copy(refs[n], refs[2 * count + n], in_s.at[n]) for n in range(count)
    ]
    leaving = [
        pltpu.make_async_copy(refs[2 * count + n], refs[count + n], out_s.at[n])
        for n in range(count)
    ]
    for copy in arriving:
        copy.start()
    for n in range(count):
        arriving[n].wait()
        leaving[n].start()
    for copy in leaving:
        copy.wait()


def per_device(
    n_row, n_col,
    pair_trunk, pair_gain, pair_weight, atom_features, atom_gain, attn_weights, token_atoms,
    window_starts, out_cotangent,
):
    band, cols, width = pair_trunk.shape
    samples, count, _ = atom_features.shape
    heads = pair_weight.shape[0]
    total = cols * n_col
    lanes = max(128, heads * band)
    ext = count + WINDOW
    half = WINDOW // 2
    hq = heads * count
    share = 4 * width // n_row
    vmem = pl.BlockSpec(memory_space=pltpu.VMEM)
    anywhere = pl.BlockSpec(memory_space=pl.ANY)
    dma = pltpu.SemaphoreType.DMA
    steps = samples // PAIRED
    hbm = pl.BlockSpec(memory_space=pltpu.HBM)
    args = [
        pair_trunk, pair_gain.reshape(1, width), pair_weight, atom_features,
        atom_gain.reshape(1, width), attn_weights, token_atoms, window_starts, out_cotangent,
    ]
    scratch = [(args[n].shape, args[n].dtype) for n in (0, 1, 2, 3, 4, 5, 6, 8)]
    later = [
        ((2, samples, count, width), BF16),
        ((samples, count, width), BF16),
        ((samples, ext, width), BF16),
        ((samples, ext, width), BF16),
        ((samples, ext, width), BF16),
        ((samples, count, width), F32),
        ((samples, count, 1), F32),
        ((samples, count, width), BF16),
        ((samples, count, width), BF16),
        ((samples, count, width), BF16),
        ((samples, ext, 2 * width), BF16),
        ((samples, count, width), F32),
        ((2, samples, half, width), BF16),
        ((2, samples, half, width), BF16),
        ((ext, hq), F32),
        ((ext, hq), F32),
        ((ext, total), BF16),
        ((hq, lanes), BF16),
        ((hq, width), BF16),
        ((lanes, width), BF16),
        ((band, cols, width), F32),
        ((band, cols, 1), F32),
        ((n_col, cols, lanes), BF16),
        ((n_col, cols, lanes), BF16),
        ((n_col, cols, lanes), BF16),
        ((n_row, share, width), BF16),
        ((n_row, share, width), BF16),
        ((n_col, share, width), F32),
        ((n_row, share, width), BF16),
        ((n_row, 8, width), F32),
        ((n_col, 8, width), F32),
    ]
    sems = [(9,), (2, steps), (2, steps), (n_col,), (n_col,), (2, steps), (2, steps), (n_col,), (n_col,),
            (n_row,), (n_row,), (n_col,), (n_col,), (n_row,), (n_row,), (n_row,), (n_row,),
            (n_col,), (n_col,)]
    outs = pl.pallas_call(
        functools.partial(kernel, n_row, n_col),
        out_shape=[
            jax.ShapeDtypeStruct((samples, count, width), BF16),
            jax.ShapeDtypeStruct((samples, count, width), F32),
            jax.ShapeDtypeStruct((band, cols, width), BF16),
            jax.ShapeDtypeStruct((4, width, width), F32),
            jax.ShapeDtypeStruct((1, width), F32),
            jax.ShapeDtypeStruct((heads, width), F32),
            jax.ShapeDtypeStruct((1, width), F32),
        ],
        in_specs=[hbm] * 9,
        out_specs=[vmem] * 7,
        scratch_shapes=[pltpu.VMEM(shape, kind) for shape, kind in scratch]
        + [pltpu.SMEM(window_starts.shape, jnp.int32)]
        + [pltpu.VMEM(shape, kind) for shape, kind in later]
        + [dma(shape) for shape in sems],
        compiler_params=pltpu.CompilerParams(
            collective_id=0, has_side_effects=True, vmem_limit_bytes=60 << 20),
    )(*args)
    outs = pl.pallas_call(
        handover,
        out_shape=[pltpu.HBM(out.shape, out.dtype) for out in outs],
        in_specs=[anywhere] * 7,
        out_specs=[anywhere] * 7,
        scratch_shapes=[pltpu.VMEM(out.shape, out.dtype) for out in outs] + [dma((7,)), dma((7,))],
        compiler_params=pltpu.CompilerParams(vmem_limit_bytes=60 << 20),
    )(*outs)
    return (outs[0], outs[1], outs[2], outs[3], outs[4].reshape(width), outs[5],
            outs[6].reshape(width))


def solution(mesh):
    atoms_at = P(None, ("row", "col"), None)
    pairs_at = P("row", "col", None)
    return jax.shard_map(
        functools.partial(per_device, mesh.shape["row"], mesh.shape["col"]),
        mesh=mesh,
        in_specs=(pairs_at, P(), P(), atoms_at, P(), P(), P(), P(("row", "col")), atoms_at),
        out_specs=(atoms_at, atoms_at, pairs_at, P(), P(), P(), P()),
        check_vma=False,
    )
```

```python
import functools
import math

import jax
import jax.numpy as jnp
from jax import lax
from jax.experimental import pallas as pl
from jax.experimental.pallas import tpu as pltpu
from jax.sharding import PartitionSpec as P

WINDOW = 128
EPS = 1e-05
MESH = pl.DeviceIdType.MESH
F32 = jnp.float32
BF16 = jnp.bfloat16
NT = (((1,), (1,)), ((), ()))
NN = (((1,), (0,)), ((), ()))
TN = (((0,), (0,)), ((), ()))
MASKED = -1e30
GROUP = 4
PAIRED = 4


def dot(a, b, dims):
    return lax.dot_general(a, b, dims, preferred_element_type=F32)


def iota(shape, dim):
    return lax.broadcasted_iota(jnp.int32, shape, dim)


def normalised(x):
    x = x.astype(F32)
    center = x - jnp.mean(x, axis=-1, keepdims=True)
    rstd = lax.rsqrt(jnp.mean(center * center, axis=-1, keepdims=True) + EPS)
    return center * rstd, rstd


def norm_back(grad, gain, xhat, rstd):
    scaled = grad * gain
    first = jnp.mean(scaled, axis=-1, keepdims=True)
    second = jnp.mean(scaled * xhat, axis=-1, keepdims=True)
    return rstd * (scaled - first - xhat * second)


def fold8(x):
    return jnp.sum(x.reshape(x.shape[0] // 8, 8, x.shape[1]), axis=0)


def kernel(
    n_row, n_col,
    trunk_h, pgain_h, pweight_h, atoms_h, again_h, weights_h, tokens_h, starts_h, cot_h,
    updated, grad_atoms, grad_pair, grad_w, grad_again, grad_pweight, grad_pgain,
    trunk, pair_gain, pair_weight, atoms, atom_gain, weights, token_atoms, cot, starts,
    halo, q_s, k_ext, v_ext, n_ext, xhat_s, rstd_s, gmix, mixed_s, dq_s, dkv_s,
    dn_own, dn_out, dn_in, tile, dt_acc, ok_s, oq_s, hmask_s, wrep_s, pxhat, prstd,
    bias_all, g_out, g_in, rs_out, rs_in, cb, ag, sm, sc,
    in_s, halo_ss, halo_rs, bias_ss, bias_rs, dn_ss, dn_rs, g_ss, g_rs,
    rs_ss, rs_rs, cb_ss, cb_rs, ag_ss, ag_rs, sm_ss, sm_rs, sc_ss, sc_rs,
):
    row = lax.axis_index("row")
    col = lax.axis_index("col")
    n_dev = n_row * n_col
    me = row * n_col + col
    up = lax.rem(me + 1, n_dev)
    down = lax.rem(me + n_dev - 1, n_dev)
    up_id = (up // n_col, lax.rem(up, n_col))
    down_id = (down // n_col, lax.rem(down, n_col))
    samples, count, width = atoms.shape
    band, cols, _ = trunk.shape
    heads = pair_weight.shape[0]
    head_dim = width // heads
    total = cols * n_col
    lanes = wrep_s.shape[0]
    ext = count + WINDOW
    half = WINDOW // 2
    hq = heads * count
    scale = 1.0 / math.sqrt(head_dim)
    band_atoms = count * n_col
    first = me * count

    has_up = me < n_dev - 1
    has_down = me > 0

    @pl.when(me == 0)
    def _():
        halo[0] = jnp.zeros(halo.shape[1:], BF16)
        dn_in[1] = jnp.zeros(dn_in.shape[1:], BF16)

    @pl.when(me == n_dev - 1)
    def _():
        halo[1] = jnp.zeros(halo.shape[1:], BF16)
        dn_in[0] = jnp.zeros(dn_in.shape[1:], BF16)

    def row_peer(d):
        return lax.rem(row + d, n_row)

    def col_peer(d):
        return lax.rem(col + d, n_col)

    loads = [
        pltpu.make_async_copy(source, target, in_s.at[n])
        for n, (source, target) in enumerate((
            (trunk_h, trunk), (pgain_h, pair_gain), (pweight_h, pair_weight),
            (again_h, atom_gain), (atoms_h, atoms), (weights_h, weights), (cot_h, cot),
            (tokens_h, token_atoms), (starts_h, starts)))
    ]
    barrier = pltpu.get_barrier_semaphore()
    pl.semaphore_signal(barrier, inc=1, device_id=up_id, device_id_type=MESH)
    pl.semaphore_signal(barrier, inc=1, device_id=down_id, device_id_type=MESH)

    @pl.loop(1, n_row)
    def _(d):
        pl.semaphore_signal(barrier, inc=1, device_id=(row_peer(d), col), device_id_type=MESH)

    @pl.loop(1, n_col)
    def _(d):
        pl.semaphore_signal(barrier, inc=1, device_id=(row, col_peer(d)), device_id_type=MESH)

    for copy in loads:
        copy.start()
    pl.semaphore_wait(barrier, n_row + n_col)

    def halo_copy(d, it, where):
        some = pl.ds(it * PAIRED, PAIRED)
        return pltpu.make_async_remote_copy(
            src_ref=atoms_h.at[some], dst_ref=halo.at[d, some], send_sem=halo_ss.at[d, it],
            recv_sem=halo_rs.at[d, it], device_id=where, device_id_type=MESH)

    @pl.loop(0, samples // PAIRED)
    def _(it):
        pl.when(has_up)(lambda: halo_copy(0, it, up_id).start())
        pl.when(has_down)(lambda: halo_copy(1, it, down_id).start())

    for copy in loads[:4]:
        copy.wait()
    again = atom_gain[...]
    pgain = pair_gain[...]

    lane_row = iota((lanes, width), 0)
    wrep = jnp.zeros((lanes, width), F32)
    for h in range(heads):
        wrep = jnp.where(lane_row // band == h, pair_weight[h : h + 1, :].astype(F32), wrep)
    wrep_s[...] = wrep.astype(BF16)

    def pair_rows(i):
        return jnp.where(lane_row % band == i, wrep_s[...].astype(F32), 0.0).astype(BF16)

    def forward_step(i, acc):
        xhat, rstd = normalised(trunk[i])
        pxhat[i] = xhat
        prstd[i] = rstd
        return acc + dot((xhat * pgain).astype(BF16), pair_rows(i), NT)

    bias = lax.fori_loop(0, band, forward_step, jnp.zeros((cols, lanes), F32), unroll=2)
    bias_all[col] = bias.astype(BF16)

    def bias_copy(peer, slot):
        return pltpu.make_async_remote_copy(
            src_ref=bias_all.at[col], dst_ref=bias_all.at[slot], send_sem=bias_ss.at[peer],
            recv_sem=bias_rs.at[slot], device_id=(row, peer), device_id_type=MESH)

    @pl.loop(1, n_col)
    def _(d):
        bias_copy(col_peer(d), col).start()

    for copy in loads[4:]:
        copy.wait()

    wqkv = jnp.concatenate([weights[0], weights[1], weights[2]], axis=1)
    wkv = jnp.concatenate([weights[1], weights[2]], axis=1)

    @pl.loop(0, samples // GROUP)
    def _(c):
        some = pl.ds(c * GROUP, GROUP)
        flat = (GROUP * count, width)
        cube = (GROUP, count, width)
        xhat, rstd = normalised(atoms[some].reshape(flat))
        normed = (xhat * again).astype(BF16)
        proj = dot(normed, wqkv, NN).astype(BF16)
        xhat_s[some] = xhat.reshape(cube)
        rstd_s[some] = rstd.reshape(GROUP, count, 1)
        n_ext[some, half : half + count] = normed.reshape(cube)
        q_s[some] = proj[:, :width].reshape(cube)
        k_ext[some, half : half + count] = proj[:, width : 2 * width].reshape(cube)
        v_ext[some, half : half + count] = proj[:, 2 * width :].reshape(cube)
        gmix[some] = dot(cot[some].reshape(flat), weights[3], NT).astype(BF16).reshape(cube)

    table = token_atoms[...].astype(F32).astype(BF16)

    def bounds(size, token_of, band_of, band_row):
        token = token_of(iota((band, size), 1))
        at = iota((band, size), 0)
        own = iota((n_row, size), 0) == band_of(iota((n_row, size), 1))
        out = []
        for strict in (True, False):
            below = (at < token) if strict else (at <= token)
            sums = dot(table, jnp.where(below, 1.0, 0.0).astype(BF16), NN)
            inner = jnp.sum(jnp.where(own, sums, 0.0), axis=0, keepdims=True)
            out.append(inner.astype(jnp.int32) + band_row(iota((1, size), 1)) * band_atoms)
        return out

    low, high = bounds(total, lambda j: j % band, lambda j: j // band, lambda j: j // band)
    key_atom = first - half + iota((ext, total), 0)
    ok_s[...] = jnp.where((key_atom >= low) & (key_atom < high), 1.0, 0.0).astype(BF16)
    low, high = bounds(lanes, lambda l: l % band, lambda l: l * 0 + row, lambda l: l * 0 + row)
    sub = iota((hq, lanes), 0)
    query_atom = first + sub % count
    same_head = (sub // count) == (iota((hq, lanes), 1) // band)
    oq_s[...] = jnp.where(
        same_head & (query_atom >= low) & (query_atom < high), 1.0, 0.0).astype(BF16)
    hmask_s[...] = jnp.where(
        iota((hq, width), 0) // count == iota((hq, width), 1) // head_dim, 1.0, 0.0).astype(BF16)

    @pl.loop(1, n_col)
    def _(d):
        peer = col_peer(d)
        bias_copy(peer, peer).wait()

    spread = dot(ok_s[...], bias_all[...].reshape(total, lanes), NN).astype(BF16)
    block = (iota((ext, hq), 1) % count) // (count // starts.shape[0])
    offset = jnp.zeros((ext, hq), jnp.int32)
    for b in range(starts.shape[0]):
        offset = jnp.where(block == b, starts[b] - (first - half), offset)
    place = iota((ext, hq), 0) - offset
    tile[...] = jnp.where(
        (place >= 0) & (place < WINDOW), dot(spread, oq_s[...], NT), MASKED)
    dt_acc[...] = jnp.zeros_like(dt_acc)

    def dn_copy(d, it, where):
        some = pl.ds(it * PAIRED, PAIRED)
        return pltpu.make_async_remote_copy(
            src_ref=dn_out.at[d, some], dst_ref=dn_in.at[d, some], send_sem=dn_ss.at[d, it],
            recv_sem=dn_rs.at[d, it], device_id=where, device_id_type=MESH)

    def by_head(full):
        masked = full * hmask_s[...].astype(F32)
        out = masked[:count]
        for h in range(1, heads):
            out = out + masked[h * count : (h + 1) * count]
        return out

    def spread_heads(x):
        return jnp.concatenate([x] * heads, axis=0) * hmask_s[...]

    @pl.loop(0, samples // PAIRED)
    def _(it):
        pl.when(has_up)(lambda: halo_copy(0, it, up_id).wait_send())
        pl.when(has_down)(lambda: halo_copy(0, it, up_id).wait_recv())
        pl.when(has_down)(lambda: halo_copy(1, it, down_id).wait_send())
        pl.when(has_up)(lambda: halo_copy(1, it, down_id).wait_recv())
        some = pl.ds(it * PAIRED, PAIRED)
        cube = (PAIRED, half, width)
        for d in range(2):
            base = d * (half + count)
            xhat, _r = normalised(halo[d, some].reshape(PAIRED * half, width))
            normed = (xhat * again).astype(BF16)
            proj = dot(normed, wkv, NN).astype(BF16)
            n_ext[some, base : base + half] = normed.reshape(cube)
            k_ext[some, base : base + half] = proj[:, :width].reshape(cube)
            v_ext[some, base : base + half] = proj[:, width:].reshape(cube)
        added = None
        for u in range(PAIRED):
            s = it * PAIRED + u
            k, v = k_ext[s], v_ext[s]
            qbd = spread_heads(q_s[s])
            gbd = spread_heads(gmix[s])
            scores = dot(k, qbd, NT) * scale + tile[...]
            grown = jnp.exp(scores - jnp.max(scores, axis=0, keepdims=True))
            probs = grown * (1.0 / jnp.sum(grown, axis=0, keepdims=True))
            probs_bf = probs.astype(BF16)
            mixed_s[s] = by_head(dot(probs_bf, v, TN)).astype(BF16)
            gprobs = dot(v, gbd, NT).astype(BF16).astype(F32)
            weighed = probs * gprobs
            gscores = weighed - probs * jnp.sum(weighed, axis=0, keepdims=True)
            added = gscores if added is None else added + gscores
            gs_bf = (gscores * scale).astype(BF16)
            gq = by_head(dot(gs_bf, k, TN)).astype(BF16)
            gk = dot(gs_bf, qbd, NN).astype(BF16)
            gv = dot(probs_bf, gbd, NN).astype(BF16)
            dq_s[s] = gq
            dkv_s[s, :, :width] = gk
            dkv_s[s, :, width:] = gv
            gn = dot(gk, weights[1], NT) + dot(gv, weights[2], NT)
            dn_out[0, s] = gn[:half].astype(BF16)
            dn_out[1, s] = gn[half + count :].astype(BF16)
            dn_own[s] = gn[half : half + count] + dot(gq, weights[0], NT)
        dt_acc[...] += added
        pl.when(has_down)(lambda: dn_copy(0, it, down_id).start())
        pl.when(has_up)(lambda: dn_copy(1, it, up_id).start())

    by_query = dot(dt_acc[...].astype(BF16), oq_s[...], NN).astype(BF16)
    g_out[...] = dot(ok_s[...], by_query, TN).astype(BF16).reshape(n_col, cols, lanes)

    def g_copy(peer, slot):
        return pltpu.make_async_remote_copy(
            src_ref=g_out.at[peer], dst_ref=g_in.at[slot], send_sem=g_ss.at[peer],
            recv_sem=g_rs.at[slot], device_id=(row, peer), device_id_type=MESH)

    @pl.loop(1, n_col)
    def _(d):
        g_copy(col_peer(d), col).start()

    g_in[col] = g_out[col]

    rows_all = samples * count
    share = rs_out.shape[1]
    own_n = n_ext[:, half : half + count].reshape(rows_all, width)
    per = width // share
    gwq = dot(own_n, dq_s[...].reshape(rows_all, width), TN)
    gwkv = dot(n_ext[...].reshape(samples * ext, width),
               dkv_s[...].reshape(samples * ext, 2 * width), TN)
    mixed_all = mixed_s[...].reshape(rows_all, width)
    gwo = dot(mixed_all, cot[...].reshape(rows_all, width), TN)
    for p, value in enumerate((gwq, gwkv[:, :width], gwkv[:, width:], gwo)):
        rs_out[p * per : (p + 1) * per] = value.astype(BF16).reshape(per, share, width)

    def rs_copy(peer, slot):
        return pltpu.make_async_remote_copy(
            src_ref=rs_out.at[peer], dst_ref=rs_in.at[slot], send_sem=rs_ss.at[peer],
            recv_sem=rs_rs.at[slot], device_id=(peer, col), device_id_type=MESH)

    @pl.loop(1, n_row)
    def _(d):
        rs_copy(row_peer(d), row).start()

    rs_in[row] = rs_out[row]

    @pl.loop(0, samples // GROUP)
    def _(c):
        some = pl.ds(c * GROUP, GROUP)
        moved = dot(mixed_s[some].reshape(GROUP * count, width), weights[3], NN)
        updated[some] = (atoms[some].astype(F32) + moved.reshape(GROUP, count, width)).astype(BF16)

    @pl.loop(1, n_col)
    def _(d):
        peer = col_peer(d)
        g_copy(peer, peer).wait()

    grad_bias = g_in[0].astype(F32)
    for c in range(1, n_col):
        grad_bias = grad_bias + g_in[c].astype(F32)
    grad_bias_t = grad_bias.T.astype(BF16)
    grad_bias = grad_bias.astype(BF16)

    def backward_step(i, carry):
        gain_acc, w_acc = carry
        xhat = pxhat[i]
        grad = dot(grad_bias, pair_rows(i), NN)
        normed = (xhat * pgain).astype(BF16)
        gain_acc = gain_acc + fold8(grad * xhat)
        w_acc = w_acc + jnp.where(lane_row % band == i, dot(grad_bias_t, normed, NN), 0.0)
        grad_pair[i] = norm_back(grad, pgain, xhat, prstd[i]).astype(BF16)
        return gain_acc, w_acc

    pgain_acc, w_acc = lax.fori_loop(
        0, band, backward_step,
        (jnp.zeros((8, width), F32), jnp.zeros((lanes, width), F32)), unroll=2)

    @pl.loop(1, n_row)
    def _(d):
        peer = row_peer(d)
        rs_copy(peer, peer).wait()

    part = rs_in[0].astype(F32)
    for r in range(1, n_row):
        part = part + rs_in[r].astype(F32)
    cb[col] = part

    def cb_copy(peer, slot):
        return pltpu.make_async_remote_copy(
            src_ref=cb.at[col], dst_ref=cb.at[slot], send_sem=cb_ss.at[peer],
            recv_sem=cb_rs.at[slot], device_id=(row, peer), device_id_type=MESH)

    @pl.loop(1, n_col)
    def _(d):
        cb_copy(col_peer(d), col).start()

    @pl.loop(0, samples // PAIRED)
    def _(it):
        pl.when(has_down)(lambda: dn_copy(0, it, down_id).wait_send())
        pl.when(has_up)(lambda: dn_copy(0, it, down_id).wait_recv())
        pl.when(has_up)(lambda: dn_copy(1, it, up_id).wait_send())
        pl.when(has_down)(lambda: dn_copy(1, it, up_id).wait_recv())

    def atom_step(c, gain_acc):
        some = pl.ds(c * GROUP, GROUP)
        flat = (GROUP * count, width)
        cube = (GROUP, count, width)
        grad = (dn_own[some] + dn_in[0, some].astype(F32) + dn_in[1, some].astype(F32)).reshape(flat)
        xhat = xhat_s[some].reshape(flat)
        back = norm_back(grad, again, xhat, rstd_s[some].reshape(GROUP * count, 1))
        grad_atoms[some] = cot[some].astype(F32) + back.reshape(cube)
        return gain_acc + fold8(grad * xhat)

    again_acc = lax.fori_loop(0, samples // GROUP, atom_step, jnp.zeros((8, width), F32))

    @pl.loop(1, n_col)
    def _(d):
        peer = col_peer(d)
        cb_copy(peer, peer).wait()

    whole = cb[0]
    for c in range(1, n_col):
        whole = whole + cb[c]
    ag[row] = whole.astype(BF16)

    def ag_copy(peer, slot):
        return pltpu.make_async_remote_copy(
            src_ref=ag.at[row], dst_ref=ag.at[slot], send_sem=ag_ss.at[peer],
            recv_sem=ag_rs.at[slot], device_id=(peer, col), device_id_type=MESH)

    small = [jnp.sum(again_acc, axis=0, keepdims=True), jnp.sum(pgain_acc, axis=0, keepdims=True)]
    for h in range(heads):
        small.append(jnp.sum(w_acc[h * band : (h + 1) * band], axis=0, keepdims=True))
    small.append(jnp.zeros((8 - len(small), width), F32))
    sm[row] = jnp.concatenate(small, axis=0)

    def sm_copy(peer, slot):
        return pltpu.make_async_remote_copy(
            src_ref=sm.at[row], dst_ref=sm.at[slot], send_sem=sm_ss.at[peer],
            recv_sem=sm_rs.at[slot], device_id=(peer, col), device_id_type=MESH)

    @pl.loop(1, n_row)
    def _(d):
        sm_copy(row_peer(d), row).start()
        ag_copy(row_peer(d), row).start()

    @pl.loop(1, n_row)
    def _(d):
        peer = row_peer(d)
        sm_copy(peer, peer).wait()

    small_part = sm[0]
    for r in range(1, n_row):
        small_part = small_part + sm[r]
    sc[col] = small_part

    def sc_copy(peer, slot):
        return pltpu.make_async_remote_copy(
            src_ref=sc.at[col], dst_ref=sc.at[slot], send_sem=sc_ss.at[peer],
            recv_sem=sc_rs.at[slot], device_id=(row, peer), device_id_type=MESH)

    @pl.loop(1, n_col)
    def _(d):
        sc_copy(col_peer(d), col).start()

    @pl.loop(1, n_row)
    def _(d):
        peer = row_peer(d)
        ag_copy(peer, peer).wait()

    for p in range(4):
        grad_w[p] = ag[p * per : (p + 1) * per].reshape(width, width).astype(F32)

    @pl.loop(1, n_col)
    def _(d):
        peer = col_peer(d)
        sc_copy(peer, peer).wait()

    sums = sc[0]
    for c in range(1, n_col):
        sums = sums + sc[c]
    grad_again[...] = sums[0:1]
    grad_pgain[...] = sums[1:2]
    grad_pweight[...] = sums[2 : 2 + heads]


def handover(*refs):
    count = (len(refs) - 2) // 3
    in_s, out_s = refs[-2:]
    arriving = [
        pltpu.make_async_copy(refs[n], refs[2 * count + n], in_s.at[n]) for n in range(count)
    ]
    leaving = [
        pltpu.make_async_copy(refs[2 * count + n], refs[count + n], out_s.at[n])
        for n in range(count)
    ]
    for copy in arriving:
        copy.start()
    for n in range(count):
        arriving[n].wait()
        leaving[n].start()
    for copy in leaving:
        copy.wait()


def per_device(
    n_row, n_col,
    pair_trunk, pair_gain, pair_weight, atom_features, atom_gain, attn_weights, token_atoms,
    window_starts, out_cotangent,
):
    band, cols, width = pair_trunk.shape
    samples, count, _ = atom_features.shape
    heads = pair_weight.shape[0]
    total = cols * n_col
    lanes = max(128, heads * band)
    ext = count + WINDOW
    half = WINDOW // 2
    hq = heads * count
    share = 4 * width // n_row
    vmem = pl.BlockSpec(memory_space=pltpu.VMEM)
    anywhere = pl.BlockSpec(memory_space=pl.ANY)
    dma = pltpu.SemaphoreType.DMA
    steps = samples // PAIRED
    hbm = pl.BlockSpec(memory_space=pltpu.HBM)
    args = [
        pair_trunk, pair_gain.reshape(1, width), pair_weight, atom_features,
        atom_gain.reshape(1, width), attn_weights, token_atoms, window_starts, out_cotangent,
    ]
    scratch = [(args[n].shape, args[n].dtype) for n in (0, 1, 2, 3, 4, 5, 6, 8)]
    later = [
        ((2, samples, count, width), BF16),
        ((samples, count, width), BF16),
        ((samples, ext, width), BF16),
        ((samples, ext, width), BF16),
        ((samples, ext, width), BF16),
        ((samples, count, width), F32),
        ((samples, count, 1), F32),
        ((samples, count, width), BF16),
        ((samples, count, width), BF16),
        ((samples, count, width), BF16),
        ((samples, ext, 2 * width), BF16),
        ((samples, count, width), F32),
        ((2, samples, half, width), BF16),
        ((2, samples, half, width), BF16),
        ((ext, hq), F32),
        ((ext, hq), F32),
        ((ext, total), BF16),
        ((hq, lanes), BF16),
        ((hq, width), BF16),
        ((lanes, width), BF16),
        ((band, cols, width), F32),
        ((band, cols, 1), F32),
        ((n_col, cols, lanes), BF16),
        ((n_col, cols, lanes), BF16),
        ((n_col, cols, lanes), BF16),
        ((n_row, share, width), BF16),
        ((n_row, share, width), BF16),
        ((n_col, share, width), F32),
        ((n_row, share, width), BF16),
        ((n_row, 8, width), F32),
        ((n_col, 8, width), F32),
    ]
    sems = [(9,), (2, steps), (2, steps), (n_col,), (n_col,), (2, steps), (2, steps), (n_col,), (n_col,),
            (n_row,), (n_row,), (n_col,), (n_col,), (n_row,), (n_row,), (n_row,), (n_row,),
            (n_col,), (n_col,)]
    outs = pl.pallas_call(
        functools.partial(kernel, n_row, n_col),
        out_shape=[
            jax.ShapeDtypeStruct((samples, count, width), BF16),
            jax.ShapeDtypeStruct((samples, count, width), F32),
            jax.ShapeDtypeStruct((band, cols, width), BF16),
            jax.ShapeDtypeStruct((4, width, width), F32),
            jax.ShapeDtypeStruct((1, width), F32),
            jax.ShapeDtypeStruct((heads, width), F32),
            jax.ShapeDtypeStruct((1, width), F32),
        ],
        in_specs=[hbm] * 9,
        out_specs=[vmem] * 7,
        scratch_shapes=[pltpu.VMEM(shape, kind) for shape, kind in scratch]
        + [pltpu.SMEM(window_starts.shape, jnp.int32)]
        + [pltpu.VMEM(shape, kind) for shape, kind in later]
        + [dma(shape) for shape in sems],
        compiler_params=pltpu.CompilerParams(
            collective_id=0, has_side_effects=True, vmem_limit_bytes=60 << 20),
    )(*args)
    outs = pl.pallas_call(
        handover,
        out_shape=[pltpu.HBM(out.shape, out.dtype) for out in outs],
        in_specs=[anywhere] * 7,
        out_specs=[anywhere] * 7,
        scratch_shapes=[pltpu.VMEM(out.shape, out.dtype) for out in outs] + [dma((7,)), dma((7,))],
        compiler_params=pltpu.CompilerParams(vmem_limit_bytes=60 << 20),
    )(*outs)
    return (outs[0], outs[1], outs[2], outs[3], outs[4].reshape(width), outs[5],
            outs[6].reshape(width))


def solution(mesh):
    atoms_at = P(None, ("row", "col"), None)
    pairs_at = P("row", "col", None)
    return jax.shard_map(
        functools.partial(per_device, mesh.shape["row"], mesh.shape["col"]),
        mesh=mesh,
        in_specs=(pairs_at, P(), P(), atoms_at, P(), P(), P(), P(("row", "col")), atoms_at),
        out_specs=(atoms_at, atoms_at, pairs_at, P(), P(), P(), P()),
        check_vma=False,
    )
```
